32 devices in a mesh: vocab: 8 (over z, x), seq: 4 (over y, core).
Axes of the slice: x: 2, y: 2, z: 4, core: 2. Of those that a mesh axis runs over, the one named last changes fastest.
Arguments:
- token_ids: int32 [3072, 4], P(None, 'seq'), may hold values from 0 to 12607
- lengths: int32 [8, 3], replicated, may hold values from 1 to 1344, 1536 in all within a row
- loss_place: int32 [512, 4], P(None, 'seq'), may hold values from 0 to 383
- targets: int32 [512, 4], P(None, 'seq'), may hold values from 0 to 12607
- loss_flag: int32 [512, 4], P(None, 'seq'), may hold values from 0 to 1, as said below
- layer_weight: float32 [15360, 1280], P(('vocab', 'seq')), may hold values from -8 to 8
- layer_first: float32 [15360, 1280], P(('vocab', 'seq')), may hold values from -0.00024414062 to 0.00024414062
- layer_second: float32 [15360, 1280], P(('vocab', 'seq')), may hold values from 8.37592e-10 to 1.1167893e-08
- rot_basis: float32 [32, 10, 128, 128], P(('vocab', 'seq')), may hold values from -1 to 1, as said below
- stat_matrix: float32 [32, 10, 128, 128], P(('vocab', 'seq')), may hold values from -1 to 1, as said below
- small_params: float32 [17920], replicated, may hold values from -2 to 2
- small_first: float32 [17920], replicated, may hold values from -0.0007324219 to 0.0007324219
- small_second: float32 [17920], replicated, may hold values from 8.37592e-09 to 1.11678936e-07
- embed_table: float32 [12608, 1280], P('vocab', 'seq'), may hold values from -2 to 2
- table_first: float32 [12608, 1280], P('vocab', 'seq'), may hold values from -0.00024414062 to 0.00024414062
- table_second: float32 [12608, 1280], P('vocab', 'seq'), may hold values from 8.37592e-10 to 1.1167893e-08
Outputs:
- loss_sum: float32 [], replicated
- loss_count: float32 [], replicated
- gradient_norm: float32 [], replicated
- layer_next: float32 [15360, 1280], P(('vocab', 'seq'))
- layer_first_next: float32 [15360, 1280], P(('vocab', 'seq'))
- layer_second_next: float32 [15360, 1280], P(('vocab', 'seq'))
- basis_next: float32 [32, 10, 128, 128], P(('vocab', 'seq'))
- stat_next: float32 [32, 10, 128, 128], P(('vocab', 'seq'))
- small_next: float32 [17920], replicated
- small_first_next: float32 [17920], replicated
- small_second_next: float32 [17920], replicated
- table_next: float32 [12608, 1280], P('vocab', 'seq')
- table_first_next: float32 [12608, 1280], P('vocab', 'seq')
- table_second_next: float32 [12608, 1280], P('vocab', 'seq')
- out_bias_grad: float32 [1280], replicated
The draws below stay inside these ranges and needn't reach their ends.
Inputs may be any that keep to these rules, and one draw needn't show every extreme that they name: Each group's lengths sum to 1536; its longest sequence has exactly 1344 positions. `loss_flag`: every loss position of group 8 - 1 counts. `rot_basis`: each block is orthogonal. `stat_matrix`: each block is symmetric with a positive diagonal larger than the sum of magnitudes of the rest of its row.
All inputs are finite; a program needn't handle non-finite values.
Results may differ from the reference program's by a relative error of at most 0.018.
Values may be sent and summed in bfloat16 or wider, within the bound.
No kernel may reach another device: no remote copies, remote signals or barrier semaphores. Data moves between devices by JAX's collectives and lax.ppermute only.
A program may use at most 384 MiB of HBM per device.

```python
import math
from functools import partial
import jax
import jax.numpy as jnp
import numpy as np
from jax import lax

D = 1280
HEADS = 20
HEAD_SIZE = 64
FF = 5120
VOCAB_DEV = 1576
BLK = 128
TOK_DEV = 384
LOSS_DEV = 64
NSEQS = 3
STEP = 5
GROUPS = 8
SEQ_PARTS = 4
VOCAB = 12608
VOCAB_LIVE = 12608
GROUP_TOK = 1536
LOSS_ROWS = 512
LAYER_ROWS = 15360
RDEV = 480
NBLK = 10
SMALL = 17920
NPARAM = 35816960
N_VOCAB = 8
N_SEQ = 4


def draw_loss_flag(key, part):
    key = jax.random.fold_in(key, 1)
    group_of = jnp.arange(LOSS_ROWS, dtype=jnp.int32) // LOSS_DEV
    spread = max(GROUPS - 1, 1)
    level = jax.random.randint(key, (LOSS_ROWS, SEQ_PARTS), 0, 3 * spread)
    limit = spread + 2 * group_of
    return (level < limit[:, None]).astype(jnp.int32)


def draw_layer_weight(key, part):
    key = jax.random.fold_in(key, 2)
    rows = jnp.arange(LAYER_ROWS, dtype=jnp.int32)
    scales = jnp.where(rows < 4 * D + FF, D ** (-0.5), FF ** (-0.5))
    base = jnp.clip(jax.random.normal(key, (LAYER_ROWS, D), jnp.float32), -6.0, 6.0)
    return base * scales[:, None].astype(jnp.float32)


def draw_small_params(key, part):
    key = jax.random.fold_in(key, 3)
    index = jnp.arange(SMALL, dtype=jnp.int32)
    noise = jnp.clip(jax.random.normal(key, (SMALL,), jnp.float32), -4.0, 4.0)
    start = 4 * D + FF
    gains = (index >= start) & (index < start + D) | (index >= start + 2 * D) & (index < start + 3 * D) | (index >= start + 4 * D) & (index < start + 5 * D)
    return jnp.where(gains, 0.15 * noise, 0.02 * noise)


def draw_embed_table(key, part):
    key = jax.random.fold_in(key, 4)
    shard = (jnp.arange(VOCAB, dtype=jnp.int32) // VOCAB_DEV).astype(jnp.float32)
    spread = max(GROUPS - 1, 1)
    base = jnp.clip(jax.random.normal(key, (VOCAB, D), jnp.float32), -6.0, 6.0)
    rise = 2.0
    scales = (1.0 + rise * shard / spread) * D ** (-0.5)
    return base * scales[:, None]


def draw_rot_basis(key, part):
    key = jax.random.fold_in(key, 5)
    vector = jax.random.normal(key, (GROUPS * SEQ_PARTS, NBLK, BLK), jnp.float32) + 0.5
    length = jnp.sum(vector * vector, -1)
    eye_mat = jnp.eye(BLK, dtype=jnp.float32)
    return eye_mat - 2.0 * vector[..., :, None] * vector[..., None, :] / length[..., None, None]


def draw_stat_matrix(key, part):
    key = jax.random.fold_in(key, 6)
    first_key, second_key = jax.random.split(key)
    level = 0.05 * RDEV / NPARAM
    diagonal = level * jnp.exp(jax.random.uniform(first_key, (GROUPS * SEQ_PARTS, NBLK, BLK), jnp.float32, 0.0, 1.3862944))
    border = jax.random.uniform(second_key, (GROUPS * SEQ_PARTS, NBLK, BLK, BLK), jnp.float32, -1.0, 1.0) * (0.6 * level / BLK)
    border = 0.5 * (border + jnp.swapaxes(border, -1, -2))
    eye_mat = jnp.eye(BLK, dtype=jnp.float32)
    return border * (1.0 - eye_mat) + diagonal[..., None] * eye_mat


def with_ends(entries, stream_key, smallest, high):
    longest = entries.shape.index(max(entries.shape))
    spots = []
    for shift in (0, 1):
        where = [jax.random.randint(jax.random.fold_in(stream_key, axis), (), 0, length) for axis, length in enumerate(entries.shape)]
        where[longest] = (where[longest] + shift) % entries.shape[longest]
        spots.append(tuple(where))
    return entries.at[spots[0]].set(smallest).at[spots[1]].set(high)


def levels(stream_key, extent, shards, smallest, top_value):
    loudness = 1.0
    for axis_at, blocks in shards:
        draws = jax.random.uniform(jax.random.fold_in(jax.random.fold_in(stream_key, 6), axis_at), (blocks,), jnp.float32, smallest / len(shards), top_value / len(shards))
        loudness = loudness * jnp.repeat(jnp.exp(draws), extent[axis_at] // blocks).reshape((-1,) + (1,) * (len(extent) - 1 - axis_at))
    return loudness


def rank_bounds(number_of, skew):
    loads = [(1 << 20) // math.isqrt(rank ** skew) + 1 for rank in range(1, number_of + 1)]
    scale = 1 + sum(loads) // (1 << 30)
    return np.cumsum(np.array([max(1, weight // scale) for weight in loads]))


def ranked(own_key, shape, count, skew):
    grid = rank_bounds(count, skew)
    pick = jax.random.randint(jax.random.fold_in(own_key, 1), shape, 0, int(grid[count - 1]))
    rank = jnp.searchsorted(jnp.asarray(grid, jnp.int32), pick, side="right")
    return jax.random.permutation(jax.random.fold_in(own_key, 2), count)[rank].astype(jnp.int32)


def split_up(amount, total, most, slope):
    weights = [(1 << 20) // math.isqrt(standing ** slope) + 1 for standing in range(2, amount + 1)]
    surplus, counts = total - most - (amount - 1), [1] * (amount - 1)
    while surplus > 0:
        candidates = [i for i in range(amount - 1) if counts[i] < most]
        pool, left = sum([weights[i] for i in candidates]), surplus
        for i in candidates:
            extra = min(most - counts[i], max(1, left * weights[i] // pool), surplus)
            counts[i] = counts[i] + extra
            surplus = surplus - extra
    return np.array([most] + counts)


def ragged(rng, number_of, total, most, lean):
    if number_of == 2:
        one = jax.random.randint(rng, (), max(1, total - most), min(most, total - 1) + 1)
        return jnp.stack([one, total - one])
    sizes = jnp.asarray(split_up(number_of, total, most, lean), jnp.int32)
    twos = (number_of - 1) // 2
    giver, sink = sizes[1:1 + 2 * twos:2], sizes[2:2 + 2 * twos:2]
    margin = jnp.minimum(giver - 1, most - sink)
    shifted = jax.random.randint(jax.random.fold_in(rng, 1), (twos,), 0, 1 << 20) % (margin + 1)
    sizes = sizes.at[1:1 + 2 * twos:2].set(giver - shifted).at[2:2 + 2 * twos:2].set(sink + shifted)
    return sizes[jax.random.permutation(jax.random.fold_in(rng, 2), number_of)]


def bell_draw(rng, extent, width, reach, cuts=(), kind=jnp.bfloat16):
    loudness = levels(rng, extent, cuts, -0.22, 0.18) if cuts else 1.0
    result = jax.random.normal(rng, extent, jnp.float32) * width * loudness
    return jnp.minimum(jnp.maximum(result, -reach), reach).astype(kind)


def setup_inputs(seed: int = 0) -> dict:
    arg_keys = jax.random.split(jax.random.key(seed), 17)
    return {
        "token_ids": with_ends(ranked(arg_keys[0], (GROUPS * TOK_DEV, SEQ_PARTS), VOCAB_LIVE, 2), jax.random.fold_in(arg_keys[0], 3), 0, VOCAB_LIVE - 1).astype(jnp.int32),
        "lengths": jax.vmap(lambda own: ragged(own, NSEQS, GROUP_TOK, GROUP_TOK - TOK_DEV // 2, 2))(jax.random.split(arg_keys[1], GROUPS)).reshape((GROUPS, NSEQS)).astype(jnp.int32),
        "loss_place": with_ends(jax.random.randint(arg_keys[2], (LOSS_ROWS, SEQ_PARTS), 0, TOK_DEV), jax.random.fold_in(arg_keys[2], 1), 0, TOK_DEV - 1).astype(jnp.int32),
        "targets": with_ends(ranked(arg_keys[3], (LOSS_ROWS, SEQ_PARTS), VOCAB_LIVE, 2), jax.random.fold_in(arg_keys[3], 3), 0, VOCAB_LIVE - 1).astype(jnp.int32),
        "loss_flag": draw_loss_flag(jax.random.fold_in(arg_keys[16], 71), 0),
        "layer_weight": draw_layer_weight(jax.random.fold_in(arg_keys[16], 71), 0),
        "layer_first": bell_draw(arg_keys[6], (LAYER_ROWS, D), (0.1 * NPARAM ** -0.5), 0.00024414062, ((0, 32),), jnp.float32),
        "layer_second": jnp.clip(jnp.exp(math.log(1.1167893276819996e-08) - 2.5902672 * jax.random.uniform(arg_keys[7], (LAYER_ROWS, D), jnp.float32) ** levels(arg_keys[7], (LAYER_ROWS, D), ((0, 32),), -0.2, 0.2)), 8.375919957614997e-10, 1.1167893276819996e-08),
        "rot_basis": draw_rot_basis(jax.random.fold_in(arg_keys[16], 71), 0),
        "stat_matrix": draw_stat_matrix(jax.random.fold_in(arg_keys[16], 71), 0),
        "small_params": draw_small_params(jax.random.fold_in(arg_keys[16], 71), 0),
        "small_first": bell_draw(arg_keys[11], (SMALL,), (0.3 * NPARAM ** -0.5), 0.0007324219, (), jnp.float32),
        "small_second": jnp.clip(jnp.exp(jax.random.uniform(arg_keys[12], (SMALL,), jnp.float32, math.log(8.375920401704207e-09), math.log(1.1167893632091364e-07))), 8.375920401704207e-09, 1.1167893632091364e-07),
        "embed_table": draw_embed_table(jax.random.fold_in(arg_keys[16], 71), 0),
        "table_first": bell_draw(arg_keys[14], (VOCAB, D), (0.1 * NPARAM ** -0.5), 0.00024414062, ((0, 8), (1, 4)), jnp.float32),
        "table_second": jnp.clip(jnp.exp(math.log(1.1167893276819996e-08) - 2.5902672 * jax.random.uniform(arg_keys[15], (VOCAB, D), jnp.float32) ** levels(arg_keys[15], (VOCAB, D), ((0, 8), (1, 4)), -0.2, 0.2)), 8.375919957614997e-10, 1.1167893276819996e-08),
    }


NORM_EPS = 1e-05
BETA_ONE = 0.9
BETA_TWO = 0.95
BETA_STAT = 0.95
ADAM_EPS = 1e-08
WEIGHT_DECAY = 0.1
RATE_LAYER = 0.025
RATE_SMALL = 0.08
RATE_TABLE = 0.04
MASKED = -1e+30
HIGHEST = lax.Precision.HIGHEST

@jax.custom_vjp
def low(v):
    return lax.optimization_barrier(v.astype(jnp.bfloat16)).astype(jnp.float32)

@jax.custom_vjp
def low_back(v):
    return v

def low_keep(v):
    return (low(v), None)

def low_pass(kept, grad):
    return (grad,)

def back_keep(v):
    return (v, None)

def back_low(kept, grad):
    return (low(grad),)
low.defvjp(low_keep, low_pass)
low_back.defvjp(back_keep, back_low)

def layer_norm(inputs, gain, shift):
    centre = inputs - lax.optimization_barrier(jnp.mean(inputs, -1, keepdims=True))
    spread = lax.optimization_barrier(jnp.mean(centre * centre, -1, keepdims=True))
    return centre * lax.rsqrt(spread + NORM_EPS) * (1.0 + gain) + shift

def product(left, right):
    return jnp.dot(left, right, precision=HIGHEST)

def pieces(small_params):
    bounds = [0, D, 2 * D, 3 * D, 3 * D + FF, 4 * D + FF, 5 * D + FF, 6 * D + FF, 7 * D + FF, 8 * D + FF, 9 * D + FF, 10 * D + FF]
    return [small_params[bounds[place_id]:bounds[place_id + 1]] for place_id in range(11)]

def attention(queries, key_rows, values, segments):
    length = queries.shape[0]
    block_len = min(512, length)
    positions = jnp.arange(length, dtype=jnp.int32)

    def one_block(block_id):
        offset = block_id * block_len
        query_blk = lax.dynamic_slice_in_dim(queries, offset, block_len, 0)
        query_pos = offset + jnp.arange(block_len, dtype=jnp.int32)
        query_seg = lax.dynamic_slice_in_dim(segments, offset, block_len, 0)
        scores = low_back(jnp.einsum('qhe,khe->hqk', query_blk, key_rows, precision=HIGHEST) * HEAD_SIZE ** (-0.5))
        allowed = (query_seg[:, None] == segments[None, :]) & (positions[None, :] <= query_pos[:, None])
        scores = jnp.where(allowed[None], scores, MASKED)
        chance = low(jax.nn.softmax(scores, axis=-1))
        return jnp.einsum('hqk,khe->qhe', chance, values, precision=HIGHEST)
    mixture = lax.map(jax.checkpoint(one_block), jnp.arange(length // block_len, dtype=jnp.int32))
    return mixture.reshape(length, -1)

def group_forward(low_weights, low_table, small_params, group_ids, group_lengths, group_pos):
    bias_q, bias_v, bias_out, bias_up, bias_down, gain_one, shift_one, gain_two, shift_two, gain_final, shift_final = pieces(small_params)
    length = group_ids.shape[0]
    positions = jnp.arange(length, dtype=jnp.int32)
    bounds = jnp.cumsum(group_lengths)[:-1]
    segments = lax.optimization_barrier(jnp.sum((positions[:, None] >= bounds[None, :]).astype(jnp.int32), 1))
    embedded = low_back(jnp.take(low_table, group_ids, axis=0))
    normed = low(layer_norm(embedded, gain_one, shift_one))
    joined = product(normed, low_weights[:3 * D].T) + jnp.concatenate([bias_q, jnp.zeros((D,), jnp.float32), bias_v])
    joined = low_back(low(joined))
    queries = joined[:, :D].reshape(length, HEADS, HEAD_SIZE)
    key_rows = joined[:, D:2 * D].reshape(length, HEADS, HEAD_SIZE)
    values = joined[:, 2 * D:].reshape(length, HEADS, HEAD_SIZE)
    mixed = low_back(low(attention(queries, key_rows, values, segments)))
    branch = low_back(product(mixed, low_weights[3 * D:4 * D].T) + bias_out)
    middle = embedded + branch
    normed_two = low(layer_norm(middle, gain_two, shift_two))
    hidden = low_back(product(normed_two, low_weights[4 * D:4 * D + FF].T) + bias_up)
    active = low(jax.nn.gelu(hidden, approximate=True))
    output = low_back(product(active, low_weights[4 * D + FF:]) + bias_down)
    final_out = layer_norm(middle + output, gain_final, shift_final)
    return jnp.take(final_out, group_pos, axis=0)

def adam_update(weight, first_mom, second, gradient, step_rate):
    first_mom = BETA_ONE * first_mom + (1.0 - BETA_ONE) * gradient
    second = BETA_TWO * second + (1.0 - BETA_TWO) * gradient * gradient
    direction = first_mom / (1.0 - BETA_ONE ** STEP) / (jnp.sqrt(second / (1.0 - BETA_TWO ** STEP)) + ADAM_EPS)
    return (weight - step_rate * (direction + WEIGHT_DECAY * weight), first_mom, second)

def rotated_update(weight, first_mom, second, gradient, stat, basis):
    owners = basis.shape[0]
    blocks = basis.shape[1]
    block_len = basis.shape[2]
    shaped = gradient.reshape(owners, -1, blocks, block_len)
    turned = jnp.einsum('arbi,abij->arbj', shaped, basis, precision=HIGHEST).reshape(gradient.shape)
    first_mom = BETA_ONE * first_mom + (1.0 - BETA_ONE) * turned
    second = BETA_TWO * second + (1.0 - BETA_TWO) * turned * turned
    direction = first_mom / (1.0 - BETA_ONE ** STEP) / (jnp.sqrt(second / (1.0 - BETA_TWO ** STEP)) + ADAM_EPS)
    back = jnp.einsum('arbj,abij->arbi', direction.reshape(shaped.shape), basis, precision=HIGHEST).reshape(weight.shape)
    weight_next = weight - RATE_LAYER * (back + WEIGHT_DECAY * weight)
    stat_next = BETA_STAT * stat + (1.0 - BETA_STAT) * jnp.einsum('arbi,arbj->abij', shaped, shaped, precision=HIGHEST)
    spanned = jnp.einsum('abij,abjk->abik', stat_next, basis, precision=HIGHEST)
    gram_mat = jnp.einsum('abij,abik->abjk', spanned, spanned, precision=HIGHEST)
    lower_tri = jnp.linalg.cholesky(gram_mat).reshape(-1, block_len, block_len)
    solved = jax.vmap(partial(jax.scipy.linalg.solve_triangular, lower=True))(lower_tri, jnp.swapaxes(spanned, -1, -2).reshape(-1, block_len, block_len))
    basis_next = jnp.swapaxes(solved, -1, -2).reshape(basis.shape)
    return (weight_next, first_mom, second, basis_next, stat_next)

def reference(token_ids, lengths, loss_place, targets, loss_flag, layer_weight, layer_first, layer_second, rot_basis, stat_matrix, small_params, small_first, small_second, embed_table, table_first, table_second):
    groups = N_VOCAB
    part_count = N_SEQ
    group_ids = token_ids.reshape(groups, TOK_DEV, part_count).transpose(0, 2, 1).reshape(groups, part_count * TOK_DEV)
    offsets = jnp.arange(part_count, dtype=jnp.int32) * TOK_DEV
    group_pos = (loss_place.reshape(groups, LOSS_DEV, part_count) + offsets[None, None, :]).reshape(groups, LOSS_DEV * part_count)
    flat_targets = targets.reshape(-1)
    flat_on = loss_flag.reshape(-1).astype(jnp.float32)
    row_count = flat_targets.shape[0]
    block_rows = min(512, row_count)
    live = jnp.arange(VOCAB, dtype=jnp.int32) < VOCAB_LIVE

    def objective(weights, small_vals, table_vals):
        low_weights = low(weights)
        low_table = low(table_vals)

        def one_group(inputs):
            return group_forward(low_weights, low_table, small_vals, inputs[0], inputs[1], inputs[2])
        chosen = lax.map(jax.checkpoint(one_group), (group_ids, lengths, group_pos))
        head_in = low(chosen.reshape(-1, D))

        def loss_block(block_id):
            offset = block_id * block_rows
            rows_in = lax.dynamic_slice_in_dim(head_in, offset, block_rows, 0)
            wanted = lax.dynamic_slice_in_dim(flat_targets, offset, block_rows, 0)
            counted = lax.dynamic_slice_in_dim(flat_on, offset, block_rows, 0)
            logits = low_back(product(rows_in, low_table.T))
            logits = jnp.where(live[None, :], logits, MASKED)
            peak_val = lax.optimization_barrier(jnp.max(logits, -1, keepdims=True))
            logsum = peak_val[:, 0] + jnp.log(lax.optimization_barrier(jnp.sum(jnp.exp(logits - peak_val), -1)))
            picked = jnp.take_along_axis(logits, wanted[:, None], 1)[:, 0]
            return jnp.sum(counted * (logsum - picked))
        return jnp.sum(lax.map(jax.checkpoint(loss_block), jnp.arange(row_count // block_rows, dtype=jnp.int32)))
    loss_sum, pullback = jax.vjp(objective, layer_weight, small_params, embed_table)
    grad_layer, grad_small, grad_table = pullback(jnp.ones_like(loss_sum))
    loss_count = jnp.sum(flat_on)
    squares = jnp.sum(grad_layer * grad_layer) + jnp.sum(grad_small * grad_small) + jnp.sum(grad_table * grad_table)
    gradient_norm = jnp.sqrt(squares)
    factor = 1.0 / jnp.maximum(gradient_norm, 1.0)
    out_bias_grad = factor * grad_small[2 * D:3 * D]
    layer_next, layer_first_next, layer_second_next, basis_next, stat_next = rotated_update(layer_weight, layer_first, layer_second, factor * grad_layer, stat_matrix, rot_basis)
    small_next, small_first_next, small_second_next = adam_update(small_params, small_first, small_second, factor * grad_small, RATE_SMALL)
    table_next, table_first_next, table_second_next = adam_update(embed_table, table_first, table_second, factor * grad_table, RATE_TABLE)
    return (loss_sum, loss_count, gradient_norm, layer_next, layer_first_next, layer_second_next, basis_next, stat_next, small_next, small_first_next, small_second_next, table_next, table_first_next, table_second_next, out_bias_grad)
```

```python
from functools import partial

import jax
import jax.numpy as jnp
from jax import lax
from jax.experimental import pallas as pl
from jax.experimental.pallas import tpu as pltpu
from jax.sharding import Mesh, PartitionSpec as P

HEAD_SIZE = 64
VOCAB_REAL = 50257
STEP = 5


NORM_EPS = 1e-05
BETA_ONE = 0.9
BETA_TWO = 0.95
BETA_STAT = 0.95
ADAM_EPS = 1e-08
WEIGHT_DECAY = 0.1
RATE_LAYER = 0.025
RATE_SMALL = 0.08
RATE_TABLE = 0.04
MASKED = -1e30
HIGHEST = lax.Precision.HIGHEST
LANES_BOTH = (((1,), (1,)), ((), ()))
VOCAB = ("z", "w", "x")
SEQ = ("y", "core")
ALL = VOCAB + SEQ
PLANES = 4


def layer_norm(inputs, gain, shift):
    centre = inputs - jnp.mean(inputs, -1, keepdims=True)
    spread = jnp.mean(centre * centre, -1, keepdims=True)
    return centre * lax.rsqrt(spread + NORM_EPS) * (1.0 + gain) + shift


def smooth(inputs):
    return jax.nn.gelu(inputs, approximate=True)


def low_dot(left, right):
    return lax.dot_general(left, right, LANES_BOTH, preferred_element_type=jnp.float32)


def plain_dot(left, right):
    return jnp.dot(left, right, preferred_element_type=jnp.float32)


def outer_dot(left, right, kind=jnp.float32):
    return lax.dot_general(left, right, (((0,), (0,)), ((), ())), preferred_element_type=kind)


def column_sum(values):
    return jnp.sum(values.astype(jnp.float32), 0)


def pieces(small_params, model_dim, hidden_units):
    bounds = [0, model_dim, 2 * model_dim, 3 * model_dim, 3 * model_dim + hidden_units]
    for place_id in range(7):
        bounds.append(bounds[-1] + model_dim)
    return [small_params[bounds[place_id] : bounds[place_id + 1]] for place_id in range(11)]


def swap(tensor, axis):
    return lax.ppermute(tensor, axis, [(0, 1), (1, 0)])


def shift(tensor, step):
    return lax.ppermute(tensor, "z", [(i, (i + step) % PLANES) for i in range(PLANES)])


def pick(tensor, place, axis=0):
    return lax.dynamic_index_in_dim(tensor, place, axis, keepdims=False)


def added(*tensors):
    total = tensors[0].astype(jnp.float32)
    for tensor in tensors[1:]:
        total = total + tensor.astype(jnp.float32)
    return total


def lowered(*tensors):
    return added(*tensors).astype(jnp.bfloat16)


def in_order(place, own, other, axis):
    return jnp.where(
        place == 0, jnp.concatenate([own, other], axis), jnp.concatenate([other, own], axis)
    )


def split_rows(rows):
    return rows * 2 // 3


def exchange_planes(stacked):
    here = lax.axis_index("z")
    got = [pick(stacked, here)]
    for step in (3, 2, 1):
        got.append(shift(pick(stacked, (here + step) % PLANES), step))
    doubled = jnp.concatenate([part[None] for part in got + got[:3]], 0)
    return lax.dynamic_slice_in_dim(doubled, (PLANES - here) % PLANES, PLANES, 0)


def gather_pieces(piece):
    here = lax.axis_index("z")
    got = [piece] + [shift(piece, step) for step in (3, 2, 1)]
    doubled = jnp.concatenate([part[None] for part in got + got[:3]], 0)
    return lax.dynamic_slice_in_dim(doubled, (PLANES - here) % PLANES, PLANES, 0)


def gather_weights(layer_weight):
    rows, model_dim = layer_weight.shape
    quarter = rows // PLANES
    low = layer_weight.astype(jnp.bfloat16).reshape(PLANES, quarter, model_dim)
    held = exchange_planes(low)
    ways = lax.axis_size("w")
    at_x, at_y, at_c = (lax.axis_index(name) for name in ("x", "y", "core"))
    cut = split_rows(rows)
    planes = []
    for place in range(PLANES):
        mine = gather_pieces(held[place]).reshape(1, rows, model_dim)
        if ways > 1:
            mine = lax.all_gather(mine, "w", axis=0, tiled=True)
        whole = jnp.zeros((ways, 8, rows, model_dim), jnp.bfloat16)
        for offset, length, first, second in ((0, cut, "x", "y"), (cut, rows - cut, "y", "x")):
            part = mine[:, None, offset : offset + length]
            near = jnp.concatenate([part, swap(part, first)], 1)
            far = swap(near, second)
            for other, pair in ((0, near), (1, far)):
                for turned, both in ((0, pair), (1, swap(pair, "core"))):
                    for spot in (0, 1):
                        by_x, by_y = (spot, other) if first == "x" else (other, spot)
                        owner = (at_x ^ by_x) * 4 + (at_y ^ by_y) * 2 + (at_c ^ turned)
                        whole = lax.dynamic_update_slice(
                            whole, both[:, spot : spot + 1], (0, owner, offset, 0)
                        )
        planes.append(whole.reshape(-1, model_dim))
    return planes


def scatter_plane(grads):
    model_dim = grads.shape[1]
    ways = lax.axis_size("w")
    at_x, at_y, at_c, here = (lax.axis_index(name) for name in ("x", "y", "core", "z"))
    shaped = grads.reshape(ways, 2, 2, 2, -1, model_dim)
    rows = shaped.shape[4]
    cut = split_rows(rows)
    shaped = lowered(pick(shaped, at_c, 3), swap(pick(shaped, 1 - at_c, 3), "core"))
    parts = []
    for offset, length, first, second in ((0, cut, "y", "x"), (cut, rows - cut, "x", "y")):
        part = shaped[:, :, :, offset : offset + length]
        spot = {"x": at_x, "y": at_y}
        axis = 2 if first == "y" else 1
        part = lowered(
            pick(part, spot[first], axis), swap(pick(part, 1 - spot[first], axis), first)
        )
        part = lowered(pick(part, spot[second], 1), swap(pick(part, 1 - spot[second], 1), second))
        parts.append(part)
    own = jnp.concatenate(parts, 1)
    if ways > 1:
        own = lax.psum_scatter(own, "w", scatter_dimension=0, tiled=True)
    quarters = own.reshape(PLANES, rows // PLANES, model_dim)
    got = [shift(pick(quarters, (here + step) % PLANES), step) for step in (1, 2, 3)]
    return lowered(pick(quarters, here), *got)


def to_groups(theirs, mine):
    here = lax.axis_index("z")
    both = lowered(mine, swap(theirs, "x"))
    if lax.axis_size("w") > 1:
        both = lax.psum_scatter(both, "w", scatter_dimension=1, tiled=False)
    else:
        both = both[:, 0]
    got = [shift(pick(both, (here + step) % PLANES), step) for step in (1, 2, 3)]
    return added(pick(both, here), *got)


def from_groups(tensor):
    here, at_x = lax.axis_index("z"), lax.axis_index("x")
    if lax.axis_size("w") > 1:
        tensor = lax.all_gather(tensor, "w", axis=0, tiled=False)
    else:
        tensor = tensor[None]
    found = [(tensor, here, at_x)]
    for step in (1, 3, 2):
        found.append((shift(tensor, step), (here - step) % PLANES, at_x))
    return found + [(swap(got, "x"), from_z, 1 - at_x) for got, from_z, _ in found]


def total_of(values):
    for axis in ("core", "y", "x"):
        values = values + swap(values, axis)
    for step in (1, 2):
        values = values + lax.ppermute(values, "z", [(i, i ^ step) for i in range(PLANES)])
    if lax.axis_size("w") > 1:
        values = lax.psum(values, "w")
    return values


def _groups(width):
    return [(at,min(128,width-at)) for at in range(0,width,128)]

def _head_part(rows, at, wide):
    lane=lax.broadcasted_iota(jnp.int32,rows.shape,1)
    return jnp.where((lane>=at)&(lane<at+wide),rows,jnp.zeros_like(rows))

def attend_kernel(block, start_ref, q_ref, k_ref, v_ref, low_ref, out_ref, lse_ref, vt_ref):
    step=pl.program_id(0)
    width=q_ref.shape[1]
    for at,wide in _groups(width):
        @pl.when(step==0)
        def _():
            vt_ref[at:at+wide,:]=v_ref[:,at:at+wide].astype(jnp.float32).T.astype(jnp.bfloat16)
    start=start_ref[...]
    sub=lax.broadcasted_iota(jnp.int32,(block,block),0)
    lane=lax.broadcasted_iota(jnp.int32,(block,block),1)
    groups=_groups(width)
    heads=[(at,h) for at,wide in groups for h in range(wide//HEAD_SIZE)]
    parts=[]
    for at,wide in groups:
        queries=q_ref[:,at:at+wide]*jnp.bfloat16(HEAD_SIZE**-0.5)
        parts+=[_head_part(queries,h*HEAD_SIZE,HEAD_SIZE) for h in range(wide//HEAD_SIZE)]
    def chunk(place, carry, diag):
        offset=pl.multiple_of(place*block,block)
        allowed=sub>=start-offset
        if diag:
            allowed=allowed&(sub<=lane)
        fresh=[]
        scored=[]
        for i,(at,h) in enumerate(heads):
            keys=k_ref[pl.ds(offset,block),at:min(at+128,width)]
            scores=lax.dot_general(keys,parts[i],LANES_BOTH,preferred_element_type=jnp.float32)
            scored.append(jnp.where(allowed,scores,MASKED))
        for i,(at,h) in enumerate(heads):
            peak,total,acc=carry[i]
            scores=scored[i]
            higher=jnp.maximum(peak,jnp.max(scores,0,keepdims=True))
            raised=jnp.exp(scores-higher)
            shrink=jnp.exp(peak-higher)
            vt=vt_ref[i*HEAD_SIZE:(i+1)*HEAD_SIZE,pl.ds(offset,block)]
            acc=acc*shrink+jnp.dot(vt,raised.astype(jnp.bfloat16),preferred_element_type=jnp.float32)
            fresh.append((higher,total*shrink+jnp.sum(raised,0,keepdims=True),acc))
        return tuple(fresh)
    carry=tuple((jnp.full((1,block),MASKED,jnp.float32),jnp.zeros((1,block),jnp.float32),jnp.zeros((HEAD_SIZE,block),jnp.float32)) for h in heads)
    carry=lax.fori_loop(0,step,lambda c,x:chunk(c,x,False),carry)
    carry=chunk(step,carry,True)
    for at,wide in groups:
        own=carry[at//HEAD_SIZE:(at+wide)//HEAD_SIZE]
        mixed=jnp.concatenate([acc*(1.0/total) for peak,total,acc in own],0).T
        out_ref[:,at:at+wide]=mixed
        low_ref[:,at:at+wide]=mixed.astype(jnp.bfloat16)
    for i in range(len(heads)):
        peak,total,acc=carry[i]
        lse_ref[i:i+1,:]=peak+jnp.log(total)

def attend(start, queries, keys, values, block=512):
    length,width=queries.shape
    whole=lambda i:(0,0)
    rows=lambda i:(i,0)
    cols=lambda i:(0,i)
    return pl.pallas_call(
        partial(attend_kernel,block),
        grid=(length//block,),
        in_specs=[pl.BlockSpec((1,block),cols),pl.BlockSpec((block,width),rows),pl.BlockSpec((length,width),whole),pl.BlockSpec((length,width),whole)],
        out_specs=[pl.BlockSpec((block,width),rows),pl.BlockSpec((block,width),rows),pl.BlockSpec((8,block),cols)],
        out_shape=[jax.ShapeDtypeStruct((length,width),jnp.bfloat16),jax.ShapeDtypeStruct((length,width),jnp.float32),jax.ShapeDtypeStruct((8,length),jnp.float32)],
        scratch_shapes=[pltpu.VMEM((width,length),jnp.bfloat16)],
        compiler_params=pltpu.CompilerParams(vmem_limit_bytes=40<<20,dimension_semantics=("arbitrary",)),
    )(start,queries,keys,values)

def attend_back_kernel(block, start_ref, q_ref, k_ref, v_ref, do_ref, out_ref, lse_ref, dq_ref, dk_ref, dv_ref, kt_ref, dka_ref, dva_ref):
    step=pl.program_id(0)
    width=q_ref.shape[1]
    @pl.when(step==0)
    def _():
        for at,wide in _groups(width):
            kt_ref[at:at+wide,:]=k_ref[:,at:at+wide].astype(jnp.float32).T.astype(jnp.bfloat16)
        dka_ref[...]=jnp.zeros_like(dka_ref)
        dva_ref[...]=jnp.zeros_like(dva_ref)
    start=start_ref[...]
    sub=lax.broadcasted_iota(jnp.int32,(block,block),0)
    lane=lax.broadcasted_iota(jnp.int32,(block,block),1)
    temper=HEAD_SIZE**-0.5
    for at,wide in _groups(width):
        queries=q_ref[:,at:at+wide]*jnp.bfloat16(temper)
        grads=do_ref[:,at:at+wide]
        heads=range(wide//HEAD_SIZE)
        parts=[_head_part(queries,h*HEAD_SIZE,HEAD_SIZE) for h in heads]
        dparts=[_head_part(grads,h*HEAD_SIZE,HEAD_SIZE) for h in heads]
        crossed=(grads.astype(jnp.float32)*out_ref[:,at:at+wide]).T
        deltas=[jnp.sum(crossed[h*HEAD_SIZE:(h+1)*HEAD_SIZE],0,keepdims=True) for h in heads]
        lses=[lse_ref[at//HEAD_SIZE+h:at//HEAD_SIZE+h+1,:] for h in heads]
        def chunk(place, carry, diag):
            offset=pl.multiple_of(place*block,block)
            keys=k_ref[pl.ds(offset,block),at:at+wide]
            values=v_ref[pl.ds(offset,block),at:at+wide]
            allowed=sub>=start-offset
            if diag:
                allowed=allowed&(sub<=lane)
            fresh=[]
            dkey=None
            for h in heads:
                scores=lax.dot_general(keys,parts[h],LANES_BOTH,preferred_element_type=jnp.float32)
                chance=jnp.exp(jnp.where(allowed,scores,MASKED)-lses[h])
                dchance=lax.dot_general(values,dparts[h],LANES_BOTH,preferred_element_type=jnp.float32)
                dscores=(chance*(dchance-deltas[h])).astype(jnp.bfloat16)
                one=jnp.dot(dscores,parts[h],preferred_element_type=jnp.float32)
                two=jnp.dot(chance.astype(jnp.bfloat16),dparts[h],preferred_element_type=jnp.float32)
                dkey,dval=(one,two) if dkey is None else (dkey+one,dval+two)
                kt=kt_ref[at+h*HEAD_SIZE:at+(h+1)*HEAD_SIZE,pl.ds(offset,block)]
                fresh.append(carry[h]+jnp.dot(kt,dscores,preferred_element_type=jnp.float32))
            dka_ref[pl.ds(offset,block),at:at+wide]+=dkey
            dva_ref[pl.ds(offset,block),at:at+wide]+=dval
            return tuple(fresh)
        carry=tuple(jnp.zeros((HEAD_SIZE,block),jnp.float32) for h in heads)
        carry=lax.fori_loop(0,step,lambda c,x:chunk(c,x,False),carry)
        carry=chunk(step,carry,True)
        dq_ref[:,at:at+wide]=(jnp.concatenate(carry,0).T*temper).astype(jnp.bfloat16)
    @pl.when(step==pl.num_programs(0)-1)
    def _():
        dk_ref[...]=dka_ref[...].astype(jnp.bfloat16)
        dv_ref[...]=dva_ref[...].astype(jnp.bfloat16)

def attend_back(start, queries, keys, values, grad, out, lse, block=512):
    length,width=queries.shape
    whole=lambda i:(0,0)
    rows=lambda i:(i,0)
    cols=lambda i:(0,i)
    return pl.pallas_call(
        partial(attend_back_kernel,block),
        grid=(length//block,),
        in_specs=[pl.BlockSpec((1,block),cols),pl.BlockSpec((block,width),rows),pl.BlockSpec((length,width),whole),pl.BlockSpec((length,width),whole),
                  pl.BlockSpec((block,width),rows),pl.BlockSpec((block,width),rows),pl.BlockSpec((8,block),cols)],
        out_specs=[pl.BlockSpec((block,width),rows),pl.BlockSpec((length,width),whole),pl.BlockSpec((length,width),whole)],
        out_shape=[jax.ShapeDtypeStruct((length,width),jnp.bfloat16)]*3,
        scratch_shapes=[pltpu.VMEM((width,length),jnp.bfloat16),pltpu.VMEM((length,width),jnp.float32),pltpu.VMEM((length,width),jnp.float32)],
        compiler_params=pltpu.CompilerParams(vmem_limit_bytes=40<<20,dimension_semantics=("arbitrary",)),
    )(start,queries,keys,values,grad,out,lse)

def frame_kernel(gram_ref, span_ref, out_ref, work_ref, turn_ref):
    count,size,_=gram_ref.shape
    work_ref[...]=gram_ref[...]
    out_ref[...]=span_ref[...]
    sub=lax.broadcasted_iota(jnp.int32,(count,8,size),1)
    def panel(step, unused):
        top=pl.multiple_of(step*8,8)
        left=work_ref[:,pl.ds(top,8),:]
        right=out_ref[:,pl.ds(top,8),:]
        for k in range(8):
            column=left[:,:,k:k+1]
            pivot=column[:,k:k+1,:]
            inverse=lax.rsqrt(pivot)
            inverse=inverse*(1.5-0.5*pivot*inverse*inverse)
            row_left=left[:,k:k+1,:]*inverse
            row_right=right[:,k:k+1,:]*inverse
            share=column*inverse
            left=jnp.where(sub>k,left-share*row_left,jnp.where(sub==k,row_left,left))
            right=jnp.where(sub>k,right-share*row_right,jnp.where(sub==k,row_right,right))
        out_ref[:,pl.ds(top,8),:]=right
        for b in range(count):
            spread=jnp.concatenate([left[b],jnp.zeros((size-8,size),jnp.float32)],0)
            turn_ref[b]=spread.T
        turned_left=pltpu.roll(left.reshape(count*8,size),size-8,1).reshape(count,8,size)
        def trail(place, unused):
            row=pl.multiple_of(place*8,8)
            shares=turn_ref[:,pl.ds(pl.multiple_of(row-top,8),8),:]
            below_left=pltpu.roll(work_ref[:,pl.ds(row,8),:].reshape(count*8,size),size-8,1).reshape(count,8,size)
            below_right=out_ref[:,pl.ds(row,8),:]
            for k in range(8):
                share=shares[:,:,k:k+1]
                below_left=below_left-share*turned_left[:,k:k+1,:]
                below_right=below_right-share*right[:,k:k+1,:]
            work_ref[:,pl.ds(row,8),:]=below_left
            out_ref[:,pl.ds(row,8),:]=below_right
            return unused
        return lax.fori_loop(step+1,size//8,trail,unused)
    lax.fori_loop(0,size//8,panel,0)

def frame(gram, span):
    return pl.pallas_call(
        frame_kernel,
        out_shape=jax.ShapeDtypeStruct(gram.shape,jnp.float32),
        scratch_shapes=[pltpu.VMEM(gram.shape,jnp.float32),pltpu.VMEM(gram.shape,jnp.float32)],
        compiler_params=pltpu.CompilerParams(vmem_limit_bytes=40<<20),
    )(gram,span)


def adam_update(weight, first_mom, second, gradient, step_rate):
    first_mom = BETA_ONE * first_mom + (1.0 - BETA_ONE) * gradient
    second = BETA_TWO * second + (1.0 - BETA_TWO) * gradient * gradient
    direction = (
        first_mom / (1.0 - BETA_ONE**STEP) / (jnp.sqrt(second / (1.0 - BETA_TWO**STEP)) + ADAM_EPS)
    )
    return (weight - step_rate * (direction + WEIGHT_DECAY * weight), first_mom, second)


def rotated_update(weight, first_mom, second, gradient, factor, stat, basis):
    blocks, block_len = basis.shape[1], basis.shape[2]
    shaped = gradient.reshape(-1, blocks, block_len)
    frames, stats = basis[0], stat[0]
    turned = factor * jnp.einsum("rbi,bij->rbj", shaped, frames, precision=HIGHEST).reshape(
        gradient.shape
    )
    outer = jnp.einsum("rbi,rbj->bij", shaped, shaped, precision=HIGHEST)
    first_mom = BETA_ONE * first_mom + (1.0 - BETA_ONE) * turned
    second = BETA_TWO * second + (1.0 - BETA_TWO) * turned * turned
    direction = (
        first_mom / (1.0 - BETA_ONE**STEP) / (jnp.sqrt(second / (1.0 - BETA_TWO**STEP)) + ADAM_EPS)
    )
    back = jnp.einsum(
        "rbj,bij->rbi", direction.reshape(shaped.shape), frames, precision=HIGHEST
    ).reshape(weight.shape)
    weight_next = weight - RATE_LAYER * (back + WEIGHT_DECAY * weight)
    stat_next = BETA_STAT * stats + (1.0 - BETA_STAT) * (factor * factor) * outer
    spanned = jnp.einsum("bij,bjk->bik", stat_next, frames, precision=HIGHEST)
    gram = jnp.einsum("bij,bik->bjk", spanned, spanned, precision=HIGHEST)
    solved = frame(gram, jnp.swapaxes(spanned, 1, 2))
    return (weight_next, first_mom, second, jnp.swapaxes(solved, 1, 2)[None], stat_next[None])


def body(
    token_ids,
    lengths,
    loss_place,
    targets,
    loss_flag,
    layer_weight,
    layer_first,
    layer_second,
    rot_basis,
    stat_matrix,
    small_params,
    small_first,
    small_second,
    embed_table,
    table_first,
    table_second,
):
    group_id = lax.axis_index(VOCAB)
    groups = lax.axis_size(VOCAB)
    part_count = lax.axis_size(SEQ)
    ways = lax.axis_size("w")
    at_x, at_y, at_c = (lax.axis_index(name) for name in ("x", "y", "core"))
    tok_rows = token_ids.shape[0] // groups
    loss_rows = loss_place.shape[0] // groups
    vocab_rows, slice_width = embed_table.shape
    vocab_live = min(groups * vocab_rows, VOCAB_REAL)
    model_dim = layer_weight.shape[1]
    hidden_units = small_params.shape[0] - 10 * model_dim
    head_width = model_dim // part_count
    length = part_count * tok_rows
    (
        bias_q,
        bias_v,
        bias_out,
        bias_up,
        bias_down,
        gain_one,
        shift_one,
        gain_two,
        shift_two,
        gain_final,
        shift_final,
    ) = pieces(small_params, model_dim, hidden_units)

    table_low = embed_table.astype(jnp.bfloat16)
    table_y = swap(table_low, "y")
    table_near = in_order(at_c, table_low, swap(table_low, "core"), 1)
    planes = gather_weights(layer_weight)
    table_far = in_order(at_c, table_y, swap(table_y, "core"), 1)
    table_full = in_order(at_y, table_near, table_far, 1)

    local_ids = (token_ids[:, 0] - group_id * vocab_rows).reshape(PLANES, ways, 2, tok_rows)
    row_range = jnp.arange(vocab_rows, dtype=jnp.int32)

    def looked_up(ids, rows_of):
        hot = (ids.reshape(-1)[:, None] == row_range[None, :]).astype(jnp.bfloat16)
        got = plain_dot(hot, rows_of).astype(jnp.bfloat16)
        return got.reshape(ids.shape + (rows_of.shape[1],))

    halves = []
    for rows_of in (table_near, table_far):
        chunks = []
        for at in range(0, tok_rows, tok_rows // 2):
            ids = local_ids[..., at : at + tok_rows // 2]
            chunks.append(
                to_groups(
                    looked_up(pick(ids, 1 - at_x, 2), rows_of),
                    looked_up(pick(ids, at_x, 2), rows_of),
                )
            )
        halves.append(jnp.concatenate(chunks, 0))
    embedded = in_order(at_y, halves[0], halves[1], 1)

    group_lengths = jnp.take(lengths, group_id, axis=0)
    bounds = jnp.cumsum(group_lengths)[:-1]
    positions = jnp.arange(length, dtype=jnp.int32)
    starts = jnp.max(
        jnp.where(positions[:, None] >= bounds[None, :], bounds[None, :], 0), 1
    ).astype(jnp.int32)[None]

    normed_low = layer_norm(embedded, gain_one, shift_one).astype(jnp.bfloat16)
    joined = low_dot(normed_low, planes[0]) + jnp.concatenate(
        [bias_q, jnp.zeros_like(bias_q), bias_v]
    )
    joined_heads = lax.all_to_all(
        joined.astype(jnp.bfloat16).reshape(tok_rows, 3, part_count, head_width),
        SEQ,
        split_axis=2,
        concat_axis=0,
        tiled=True,
    )
    queries, key_rows, values = (joined_heads[:, at, 0] for at in range(3))
    mixture, mixture_wide, logsum = attend(starts, queries, key_rows, values)
    mixed_low = lax.all_to_all(
        mixture.reshape(part_count, tok_rows, 1, head_width),
        SEQ,
        split_axis=0,
        concat_axis=2,
        tiled=True,
    ).reshape(tok_rows, model_dim)
    half = planes[1].shape[0] - model_dim
    rest = hidden_units - half
    project_out, expand_one = planes[1][:model_dim], planes[1][model_dim:]
    expand_two, reduce_one = planes[2][:rest], planes[2][rest:]
    reduce_two = planes[3]
    reduce_cut = reduce_one.shape[0]
    middle = embedded + low_dot(mixed_low, project_out) + bias_out
    normed_two_low = layer_norm(middle, gain_two, shift_two).astype(jnp.bfloat16)
    hidden_one = low_dot(normed_two_low, expand_one) + bias_up[:half]
    hidden_two = low_dot(normed_two_low, expand_two) + bias_up[half:]
    hidden = jnp.concatenate([hidden_one, hidden_two], 1)
    active_low = smooth(hidden).astype(jnp.bfloat16)
    residual_out = (
        middle
        + plain_dot(active_low[:, :reduce_cut], reduce_one)
        + plain_dot(active_low[:, reduce_cut:], reduce_two)
        + bias_down
    )
    final_out = layer_norm(residual_out, gain_final, shift_final)
    own_pos = lax.dynamic_slice_in_dim(loss_place[:, 0], group_id * loss_rows, loss_rows, 0)
    pos_hot = own_pos[:, None] == jnp.arange(tok_rows, dtype=jnp.int32)[None, :]
    chosen = plain_dot(pos_hot.astype(jnp.bfloat16), final_out.astype(jnp.bfloat16)).astype(
        jnp.bfloat16
    )

    def whole_groups(tensor, kinds):
        found = from_groups(tensor)
        gathered = jnp.zeros((PLANES, ways, 2) + tensor.shape, kinds)
        for got, from_z, from_x in found:
            gathered = lax.dynamic_update_slice(
                gathered, got[None, :, None], (from_z, 0, from_x) + (0,) * tensor.ndim
            )
        return gathered.reshape((groups,) + tensor.shape)

    head_rows = whole_groups(chosen, jnp.bfloat16).reshape(groups * loss_rows, model_dim)
    logits = low_dot(head_rows, table_full)
    if groups * vocab_rows > vocab_live:
        row_ids = group_id * vocab_rows + row_range
        logits = jnp.where((row_ids < vocab_live)[None, :], logits, MASKED)
    target_local = targets[:, 0] - group_id * vocab_rows
    target_hot = row_range[None, :] == target_local[:, None]
    target_part = jnp.sum(jnp.where(target_hot, logits, 0.0), 1)
    local_peak = jnp.max(logits, 1)
    local_sum = jnp.sum(jnp.exp(logits - local_peak[:, None]), 1)
    everyone = whole_groups(jnp.stack([local_peak, local_sum, target_part]), jnp.float32)
    peak_all = jnp.max(everyone[:, 0], 0)
    sum_all = jnp.sum(everyone[:, 1] * jnp.exp(everyone[:, 0] - peak_all[None]), 0)
    target_logit = jnp.sum(everyone[:, 2], 0)
    logsum_all = peak_all + jnp.log(sum_all)
    weight_rows = loss_flag[:, 0].astype(jnp.float32)
    chance = jnp.exp(logits - logsum_all[:, None])
    grad_logits = weight_rows[:, None] * (chance - target_hot.astype(jnp.float32))
    grad_low = grad_logits.astype(jnp.bfloat16)
    grad_rows = plain_dot(grad_low, table_full).astype(jnp.bfloat16)
    grad_rows = grad_rows.reshape(PLANES, ways, 2, loss_rows, model_dim)
    grad_chosen = to_groups(pick(grad_rows, 1 - at_x, 2), pick(grad_rows, at_x, 2))
    grad_final = lax.dot_general(
        pos_hot.astype(jnp.float32),
        grad_chosen,
        (((0,), (0,)), ((), ())),
        precision=HIGHEST,
        preferred_element_type=jnp.float32,
    )

    head_cols = head_rows.reshape(-1, 2, 2, slice_width)

    def table_part(by_y, by_c):
        cols = pick(pick(head_cols, at_y ^ by_y, 1), at_c ^ by_c, 1)
        return outer_dot(grad_low, cols).astype(jnp.bfloat16)

    far_sum = lowered(table_part(1, 0), swap(table_part(1, 1), "core"))
    near_sum = added(table_part(0, 0), swap(table_part(0, 1), "core"))
    head_table_grad = added(near_sum, swap(far_sum, "y"))

    is_first = group_id == 0
    loss_part = jnp.where(is_first, jnp.sum(weight_rows * (logsum_all - target_logit)), 0.0)
    count_part = jnp.where(is_first, jnp.sum(weight_rows), 0.0)
    unused, final_back = jax.vjp(layer_norm, residual_out, gain_final, shift_final)
    grad_resid, grad_gain_final, grad_shift_final = final_back(grad_final)
    resid_low = grad_resid.astype(jnp.bfloat16)
    grad_bias_down = column_sum(resid_low)
    grad_active = jnp.concatenate(
        [low_dot(resid_low, reduce_one), low_dot(resid_low, reduce_two)], 1
    )
    plane_three = outer_dot(active_low[:, reduce_cut:], resid_low, jnp.bfloat16)
    piece_three = scatter_plane(plane_three)
    unused, gelu_back = jax.vjp(smooth, hidden)
    hidden_low = gelu_back(grad_active)[0].astype(jnp.bfloat16)
    grad_bias_up = column_sum(hidden_low)
    plane_two = jnp.concatenate(
        [
            outer_dot(hidden_low[:, half:], normed_two_low, jnp.bfloat16),
            outer_dot(active_low[:, :reduce_cut], resid_low, jnp.bfloat16),
        ],
        0,
    )
    piece_two = scatter_plane(plane_two)
    unused, two_back = jax.vjp(layer_norm, middle, gain_two, shift_two)
    grad_middle_part, grad_gain_two, grad_shift_two = two_back(
        plain_dot(hidden_low[:, :half], expand_one) + plain_dot(hidden_low[:, half:], expand_two)
    )
    grad_middle = grad_resid + grad_middle_part
    middle_low = grad_middle.astype(jnp.bfloat16)
    grad_bias_out = column_sum(middle_low)
    grad_mixed = plain_dot(middle_low, project_out)
    grad_heads = lax.all_to_all(
        grad_mixed.astype(jnp.bfloat16).reshape(tok_rows, part_count, head_width),
        SEQ,
        split_axis=1,
        concat_axis=0,
        tiled=True,
    )[:, 0]
    plane_one = jnp.concatenate(
        [
            outer_dot(middle_low, mixed_low, jnp.bfloat16),
            outer_dot(hidden_low[:, :half], normed_two_low, jnp.bfloat16),
        ],
        0,
    )
    piece_one = scatter_plane(plane_one)
    grad_query, grad_keys, grad_values = attend_back(
        starts, queries, key_rows, values, grad_heads, mixture_wide, logsum
    )
    grad_joined = lax.all_to_all(
        jnp.stack([grad_query, grad_keys, grad_values], 1).reshape(
            part_count, tok_rows, 3, 1, head_width
        ),
        SEQ,
        split_axis=0,
        concat_axis=3,
        tiled=True,
    ).reshape(tok_rows, 3 * model_dim)
    unused, one_back = jax.vjp(layer_norm, embedded, gain_one, shift_one)
    grad_embed_part, grad_gain_one, grad_shift_one = one_back(plain_dot(grad_joined, planes[0]))
    rows_back = (grad_middle + grad_embed_part).astype(jnp.bfloat16)
    rows_back = lax.all_to_all(rows_back, SEQ, split_axis=1, concat_axis=0, tiled=True)
    all_ids = lax.all_gather(token_ids, SEQ, axis=1, tiled=True) - group_id * vocab_rows
    all_ids = all_ids.reshape(PLANES, ways, 2, tok_rows, part_count).swapaxes(3, 4)
    table_grad = head_table_grad
    for got, from_z, from_x in from_groups(rows_back):
        ids = pick(pick(all_ids, from_z, 0), from_x, 1).reshape(1, -1)
        hot = (row_range[:, None] == ids).astype(jnp.bfloat16)
        table_grad = table_grad + plain_dot(hot, got.reshape(-1, slice_width))
    grad_bias_q = column_sum(grad_joined[:, :model_dim])
    grad_bias_v = column_sum(grad_joined[:, 2 * model_dim :])
    piece_zero = scatter_plane(outer_dot(grad_joined, normed_low, jnp.bfloat16))
    layer_grad = (
        exchange_planes(jnp.stack([piece_zero, piece_one, piece_two, piece_three]))
        .reshape(layer_weight.shape)
        .astype(jnp.float32)
    )
    early = total_of(
        jnp.concatenate(
            [
                grad_bias_out,
                grad_bias_up,
                grad_bias_down,
                grad_gain_two,
                grad_shift_two,
                grad_gain_final,
                grad_shift_final,
                jnp.stack([loss_part, count_part]),
            ]
        )
    )
    late = total_of(jnp.concatenate([grad_bias_q, grad_bias_v, grad_gain_one, grad_shift_one]))
    cut = 2 * model_dim + hidden_units
    small_grad = jnp.concatenate([late[: 2 * model_dim], early[:cut], late[2 * model_dim :], early[cut:-2]])
    loss_sum, loss_count = early[-2], early[-1]
    squares = total_of(jnp.sum(layer_grad * layer_grad) + jnp.sum(table_grad * table_grad))
    gradient_norm = jnp.sqrt(squares + jnp.sum(small_grad * small_grad))
    factor = 1.0 / jnp.maximum(gradient_norm, 1.0)
    out_bias_grad = factor * small_grad[2 * model_dim : 3 * model_dim]
    layer_next, layer_first_next, layer_second_next, basis_next, stat_next = rotated_update(
        layer_weight, layer_first, layer_second, layer_grad, factor, stat_matrix, rot_basis
    )
    small_next, small_first_next, small_second_next = adam_update(
        small_params, small_first, small_second, factor * small_grad, RATE_SMALL
    )
    table_next, table_first_next, table_second_next = adam_update(
        embed_table, table_first, table_second, factor * table_grad, RATE_TABLE
    )
    return (
        loss_sum,
        loss_count,
        gradient_norm,
        layer_next,
        layer_first_next,
        layer_second_next,
        basis_next,
        stat_next,
        small_next,
        small_first_next,
        small_second_next,
        table_next,
        table_first_next,
        table_second_next,
        out_bias_grad,
    )


def solution(mesh):
    vocab, seq = mesh.shape["vocab"], mesh.shape["seq"]
    inner = Mesh(mesh.devices.reshape(PLANES, vocab // 8, 2, seq // 2, 2), ALL)
    in_specs = (
        P(None, SEQ),
        P(),
        P(None, SEQ),
        P(None, SEQ),
        P(None, SEQ),
        P(ALL, None),
        P(ALL, None),
        P(ALL, None),
        P(ALL, None, None, None),
        P(ALL, None, None, None),
        P(),
        P(),
        P(),
        P(VOCAB, SEQ),
        P(VOCAB, SEQ),
        P(VOCAB, SEQ),
    )
    out_specs = (
        P(),
        P(),
        P(),
        P(ALL, None),
        P(ALL, None),
        P(ALL, None),
        P(ALL, None, None, None),
        P(ALL, None, None, None),
        P(),
        P(),
        P(),
        P(VOCAB, SEQ),
        P(VOCAB, SEQ),
        P(VOCAB, SEQ),
        P(),
    )
    return jax.shard_map(body, mesh=inner, in_specs=in_specs, out_specs=out_specs, check_vma=False)
```

```python
from functools import partial

import jax
import jax.numpy as jnp
from jax import lax
from jax.experimental import pallas as pl
from jax.experimental.pallas import tpu as pltpu
from jax.sharding import Mesh, PartitionSpec as P

HEAD_SIZE = 64
VOCAB_REAL = 50257
STEP = 5


NORM_EPS = 1e-05
BETA_ONE = 0.9
BETA_TWO = 0.95
BETA_STAT = 0.95
ADAM_EPS = 1e-08
WEIGHT_DECAY = 0.1
RATE_LAYER = 0.025
RATE_SMALL = 0.08
RATE_TABLE = 0.04
MASKED = -1e30
HIGHEST = lax.Precision.HIGHEST
LANES_BOTH = (((1,), (1,)), ((), ()))
PLANE = ("za", "zb")
VOCAB = PLANE + ("w", "x")
SEQ = ("y", "core")
ALL = VOCAB + SEQ
OWNERS = ("w", "x", "y", "core")
PLANES = 4


def layer_norm(inputs, gain, shift):
    centre = inputs - jnp.mean(inputs, -1, keepdims=True)
    spread = jnp.mean(centre * centre, -1, keepdims=True)
    return centre * lax.rsqrt(spread + NORM_EPS) * (1.0 + gain) + shift


def smooth(inputs):
    return jax.nn.gelu(inputs, approximate=True)


def low_dot(left, right):
    return lax.dot_general(left, right, LANES_BOTH, preferred_element_type=jnp.float32)


def plain_dot(left, right):
    return jnp.dot(left, right, preferred_element_type=jnp.float32)


def outer_dot(left, right, kind=jnp.float32):
    return lax.dot_general(left, right, (((0,), (0,)), ((), ())), preferred_element_type=kind)


def column_sum(values):
    return jnp.sum(values.astype(jnp.float32), 0)


def pieces(small_params, model_dim, hidden_units):
    bounds = [0, model_dim, 2 * model_dim, 3 * model_dim, 3 * model_dim + hidden_units]
    for place_id in range(7):
        bounds.append(bounds[-1] + model_dim)
    return [small_params[bounds[place_id] : bounds[place_id + 1]] for place_id in range(11)]


def swap(tensor, axis):
    return lax.ppermute(tensor, axis, [(0, 1), (1, 0)])


def shift(tensor, step):
    step %= PLANES
    if step == 0:
        return tensor
    return lax.ppermute(tensor, PLANE, [(i, (i + step) % PLANES) for i in range(PLANES)])


def planes_from_here():
    return [(lax.axis_index(PLANE) + step) % PLANES for step in range(PLANES)]


def gathered_z(tensor):
    return [shift(tensor, -step) for step in range(PLANES)]


def sent_z(terms):
    return [shift(terms[step], step) for step in range(PLANES)]


def pick(tensor, place, axis=0):
    return lax.dynamic_index_in_dim(tensor, place, axis, keepdims=False)


def added(*tensors):
    total = tensors[0].astype(jnp.float32)
    for tensor in tensors[1:]:
        total = total + tensor.astype(jnp.float32)
    return total


def lowered(*tensors):
    return added(*tensors).astype(jnp.bfloat16)


def in_order(place, own, other, axis):
    return jnp.where(
        place == 0, jnp.concatenate([own, other], axis), jnp.concatenate([other, own], axis)
    )


class Order:
    def __init__(self):
        self.marks = []

    def hold(self, tensors, *earlier):
        marks = [lax.slice(t, (0,) * t.ndim, (1,) * t.ndim).reshape(()) for t in earlier]
        tensors, *marks = lax.optimization_barrier((tensors, *marks))
        self.marks += [mark.astype(jnp.float32) for mark in marks]
        return tensors

    def zero(self):
        return sum(0.0 * mark for mark in self.marks)


def flip(tensor, by_core):
    pairs = []
    for place in range(8):
        pairs.append((place, place ^ (4 if by_core[place % 2] == "x" else 2)))
    return lax.ppermute(tensor, ("x", "y", "core"), pairs)


def reduce_plane(grads):
    return lax.psum_scatter(grads, OWNERS + PLANE, scatter_dimension=0, tiled=True)


def scatter_core(grads):
    model_dim = grads.shape[1]
    at_c = lax.axis_index("core")
    shaped = grads.reshape(lax.axis_size("w"), 2, 2, 2, -1, model_dim)
    return lowered(pick(shaped, at_c, 3), swap(pick(shaped, 1 - at_c, 3), "core"))


def scatter_first(shaped):
    at_x, at_y, at_c = (lax.axis_index(name) for name in ("x", "y", "core"))
    ways, unused, unused, rows, model_dim = shaped.shape
    shaped = shaped.reshape(ways, 4, rows, model_dim)

    def half(x, y):
        spots = (jnp.where(at_c == 0, y, 2 * x), jnp.where(at_c == 0, 2 + y, 2 * x + 1))
        return jnp.stack([pick(shaped, spot, 1) for spot in spots], 1)

    return lowered(half(at_x, at_y), flip(half(1 - at_x, 1 - at_y), "yx"))


def scatter_second(pair):
    spot = jnp.where(lax.axis_index("core") == 0, lax.axis_index("x"), lax.axis_index("y"))
    own = lowered(pick(pair, spot, 1), flip(pick(pair, 1 - spot, 1), "xy"))
    if lax.axis_size("w") > 1:
        own = lax.psum_scatter(own, "w", scatter_dimension=0, tiled=True)
    return own[0]


def scatter_last(own):
    rows, model_dim = own.shape
    quarters = own.reshape(PLANES, rows // PLANES, model_dim)
    return lowered(*sent_z([pick(quarters, plane) for plane in planes_from_here()]))


def own_first(tensor, place, axis):
    return jnp.stack([pick(tensor, place, axis), pick(tensor, 1 - place, axis)])


def to_group(theirs, mine):
    both = lowered(mine, swap(theirs, "x"))
    if lax.axis_size("w") > 1:
        both = lax.psum_scatter(both, "w", scatter_dimension=1, tiled=False)
    else:
        both = both[:, 0]
    return added(both[0], swap(both[1], "za"))


def from_groups(tensor, order=None, *earlier):
    if lax.axis_size("w") > 1:
        tensor = lax.all_gather(tensor, "w", axis=0, tiled=False)
    else:
        tensor = tensor[None]
    both = [tensor, swap(tensor, "za")]
    if order is not None:
        both[1] = order.hold(both[1], *earlier)
    return jnp.stack(both + [swap(part, "x") for part in both]).reshape((2, 2) + tensor.shape)


def total_of(values):
    for name in ("core", "y", "x", "zb", "za"):
        values = values + swap(values, name)
    return lax.psum(values, "w") if lax.axis_size("w") > 1 else values


def _groups(width):
    return [(at,min(128,width-at)) for at in range(0,width,128)]

def _head_part(rows, at, wide):
    lane=lax.broadcasted_iota(jnp.int32,rows.shape,1)
    return jnp.where((lane>=at)&(lane<at+wide),rows,jnp.zeros_like(rows))

def attend_kernel(block, start_ref, q_ref, k_ref, v_ref, low_ref, out_ref, lse_ref, vt_ref):
    step=pl.program_id(0)
    width=q_ref.shape[1]
    for at,wide in _groups(width):
        @pl.when(step==0)
        def _():
            vt_ref[at:at+wide,:]=v_ref[:,at:at+wide].astype(jnp.float32).T.astype(jnp.bfloat16)
    start=start_ref[...]
    sub=lax.broadcasted_iota(jnp.int32,(block,block),0)
    lane=lax.broadcasted_iota(jnp.int32,(block,block),1)
    groups=_groups(width)
    heads=[(at,h) for at,wide in groups for h in range(wide//HEAD_SIZE)]
    parts=[]
    for at,wide in groups:
        queries=q_ref[:,at:at+wide]*jnp.bfloat16(HEAD_SIZE**-0.5)
        parts+=[_head_part(queries,h*HEAD_SIZE,HEAD_SIZE) for h in range(wide//HEAD_SIZE)]
    def chunk(place, carry, diag):
        offset=pl.multiple_of(place*block,block)
        allowed=sub>=start-offset
        if diag:
            allowed=allowed&(sub<=lane)
        fresh=[]
        scored=[]
        for i,(at,h) in enumerate(heads):
            keys=k_ref[pl.ds(offset,block),at:min(at+128,width)]
            scores=lax.dot_general(keys,parts[i],LANES_BOTH,preferred_element_type=jnp.float32)
            scored.append(jnp.where(allowed,scores,MASKED))
        for i,(at,h) in enumerate(heads):
            peak,total,acc=carry[i]
            scores=scored[i]
            higher=jnp.maximum(peak,jnp.max(scores,0,keepdims=True))
            raised=jnp.exp(scores-higher)
            shrink=jnp.exp(peak-higher)
            vt=vt_ref[i*HEAD_SIZE:(i+1)*HEAD_SIZE,pl.ds(offset,block)]
            acc=acc*shrink+jnp.dot(vt,raised.astype(jnp.bfloat16),preferred_element_type=jnp.float32)
            fresh.append((higher,total*shrink+jnp.sum(raised,0,keepdims=True),acc))
        return tuple(fresh)
    carry=tuple((jnp.full((1,block),MASKED,jnp.float32),jnp.zeros((1,block),jnp.float32),jnp.zeros((HEAD_SIZE,block),jnp.float32)) for h in heads)
    carry=lax.fori_loop(0,step,lambda c,x:chunk(c,x,False),carry)
    carry=chunk(step,carry,True)
    for at,wide in groups:
        own=carry[at//HEAD_SIZE:(at+wide)//HEAD_SIZE]
        mixed=jnp.concatenate([acc*(1.0/total) for peak,total,acc in own],0).T
        out_ref[:,at:at+wide]=mixed
        low_ref[:,at:at+wide]=mixed.astype(jnp.bfloat16)
    for i in range(len(heads)):
        peak,total,acc=carry[i]
        lse_ref[i:i+1,:]=peak+jnp.log(total)

def attend(start, queries, keys, values, block=512):
    length,width=queries.shape
    whole=lambda i:(0,0)
    rows=lambda i:(i,0)
    cols=lambda i:(0,i)
    return pl.pallas_call(
        partial(attend_kernel,block),
        grid=(length//block,),
        in_specs=[pl.BlockSpec((1,block),cols),pl.BlockSpec((block,width),rows),pl.BlockSpec((length,width),whole),pl.BlockSpec((length,width),whole)],
        out_specs=[pl.BlockSpec((block,width),rows),pl.BlockSpec((block,width),rows),pl.BlockSpec((8,block),cols)],
        out_shape=[jax.ShapeDtypeStruct((length,width),jnp.bfloat16),jax.ShapeDtypeStruct((length,width),jnp.float32),jax.ShapeDtypeStruct((8,length),jnp.float32)],
        scratch_shapes=[pltpu.VMEM((width,length),jnp.bfloat16)],
        compiler_params=pltpu.CompilerParams(vmem_limit_bytes=40<<20,dimension_semantics=("arbitrary",)),
    )(start,queries,keys,values)

def attend_back_kernel(block, start_ref, q_ref, k_ref, v_ref, do_ref, out_ref, lse_ref, dq_ref, dk_ref, dv_ref, kt_ref, dka_ref, dva_ref):
    step=pl.program_id(0)
    width=q_ref.shape[1]
    @pl.when(step==0)
    def _():
        for at,wide in _groups(width):
            kt_ref[at:at+wide,:]=k_ref[:,at:at+wide].astype(jnp.float32).T.astype(jnp.bfloat16)
        dka_ref[...]=jnp.zeros_like(dka_ref)
        dva_ref[...]=jnp.zeros_like(dva_ref)
    start=start_ref[...]
    sub=lax.broadcasted_iota(jnp.int32,(block,block),0)
    lane=lax.broadcasted_iota(jnp.int32,(block,block),1)
    temper=HEAD_SIZE**-0.5
    for at,wide in _groups(width):
        queries=q_ref[:,at:at+wide]*jnp.bfloat16(temper)
        grads=do_ref[:,at:at+wide]
        heads=range(wide//HEAD_SIZE)
        parts=[_head_part(queries,h*HEAD_SIZE,HEAD_SIZE) for h in heads]
        dparts=[_head_part(grads,h*HEAD_SIZE,HEAD_SIZE) for h in heads]
        crossed=(grads.astype(jnp.float32)*out_ref[:,at:at+wide]).T
        deltas=[jnp.sum(crossed[h*HEAD_SIZE:(h+1)*HEAD_SIZE],0,keepdims=True) for h in heads]
        lses=[lse_ref[at//HEAD_SIZE+h:at//HEAD_SIZE+h+1,:] for h in heads]
        def chunk(place, carry, diag):
            offset=pl.multiple_of(place*block,block)
            keys=k_ref[pl.ds(offset,block),at:at+wide]
            values=v_ref[pl.ds(offset,block),at:at+wide]
            allowed=sub>=start-offset
            if diag:
                allowed=allowed&(sub<=lane)
            fresh=[]
            dkey=None
            for h in heads:
                scores=lax.dot_general(keys,parts[h],LANES_BOTH,preferred_element_type=jnp.float32)
                chance=jnp.exp(jnp.where(allowed,scores,MASKED)-lses[h])
                dchance=lax.dot_general(values,dparts[h],LANES_BOTH,preferred_element_type=jnp.float32)
                dscores=(chance*(dchance-deltas[h])).astype(jnp.bfloat16)
                one=jnp.dot(dscores,parts[h],preferred_element_type=jnp.float32)
                two=jnp.dot(chance.astype(jnp.bfloat16),dparts[h],preferred_element_type=jnp.float32)
                dkey,dval=(one,two) if dkey is None else (dkey+one,dval+two)
                kt=kt_ref[at+h*HEAD_SIZE:at+(h+1)*HEAD_SIZE,pl.ds(offset,block)]
                fresh.append(carry[h]+jnp.dot(kt,dscores,preferred_element_type=jnp.float32))
            dka_ref[pl.ds(offset,block),at:at+wide]+=dkey
            dva_ref[pl.ds(offset,block),at:at+wide]+=dval
            return tuple(fresh)
        carry=tuple(jnp.zeros((HEAD_SIZE,block),jnp.float32) for h in heads)
        carry=lax.fori_loop(0,step,lambda c,x:chunk(c,x,False),carry)
        carry=chunk(step,carry,True)
        dq_ref[:,at:at+wide]=(jnp.concatenate(carry,0).T*temper).astype(jnp.bfloat16)
    @pl.when(step==pl.num_programs(0)-1)
    def _():
        dk_ref[...]=dka_ref[...].astype(jnp.bfloat16)
        dv_ref[...]=dva_ref[...].astype(jnp.bfloat16)

def attend_back(start, queries, keys, values, grad, out, lse, block=512):
    length,width=queries.shape
    whole=lambda i:(0,0)
    rows=lambda i:(i,0)
    cols=lambda i:(0,i)
    return pl.pallas_call(
        partial(attend_back_kernel,block),
        grid=(length//block,),
        in_specs=[pl.BlockSpec((1,block),cols),pl.BlockSpec((block,width),rows),pl.BlockSpec((length,width),whole),pl.BlockSpec((length,width),whole),
                  pl.BlockSpec((block,width),rows),pl.BlockSpec((block,width),rows),pl.BlockSpec((8,block),cols)],
        out_specs=[pl.BlockSpec((block,width),rows),pl.BlockSpec((length,width),whole),pl.BlockSpec((length,width),whole)],
        out_shape=[jax.ShapeDtypeStruct((length,width),jnp.bfloat16)]*3,
        scratch_shapes=[pltpu.VMEM((width,length),jnp.bfloat16),pltpu.VMEM((length,width),jnp.float32),pltpu.VMEM((length,width),jnp.float32)],
        compiler_params=pltpu.CompilerParams(vmem_limit_bytes=40<<20,dimension_semantics=("arbitrary",)),
    )(start,queries,keys,values,grad,out,lse)

def frame_kernel(gram_ref, span_ref, out_ref, work_ref, turn_ref):
    count,size,_=gram_ref.shape
    work_ref[...]=gram_ref[...]
    out_ref[...]=span_ref[...]
    sub=lax.broadcasted_iota(jnp.int32,(count,8,size),1)
    def panel(step, unused):
        top=pl.multiple_of(step*8,8)
        left=work_ref[:,pl.ds(top,8),:]
        right=out_ref[:,pl.ds(top,8),:]
        for k in range(8):
            column=left[:,:,k:k+1]
            pivot=column[:,k:k+1,:]
            inverse=lax.rsqrt(pivot)
            inverse=inverse*(1.5-0.5*pivot*inverse*inverse)
            row_left=left[:,k:k+1,:]*inverse
            row_right=right[:,k:k+1,:]*inverse
            share=column*inverse
            left=jnp.where(sub>k,left-share*row_left,jnp.where(sub==k,row_left,left))
            right=jnp.where(sub>k,right-share*row_right,jnp.where(sub==k,row_right,right))
        out_ref[:,pl.ds(top,8),:]=right
        for b in range(count):
            spread=jnp.concatenate([left[b],jnp.zeros((size-8,size),jnp.float32)],0)
            turn_ref[b]=spread.T
        turned_left=pltpu.roll(left.reshape(count*8,size),size-8,1).reshape(count,8,size)
        def trail(place, unused):
            row=pl.multiple_of(place*8,8)
            shares=turn_ref[:,pl.ds(pl.multiple_of(row-top,8),8),:]
            below_left=pltpu.roll(work_ref[:,pl.ds(row,8),:].reshape(count*8,size),size-8,1).reshape(count,8,size)
            below_right=out_ref[:,pl.ds(row,8),:]
            for k in range(8):
                share=shares[:,:,k:k+1]
                below_left=below_left-share*turned_left[:,k:k+1,:]
                below_right=below_right-share*right[:,k:k+1,:]
            work_ref[:,pl.ds(row,8),:]=below_left
            out_ref[:,pl.ds(row,8),:]=below_right
            return unused
        return lax.fori_loop(step+1,size//8,trail,unused)
    lax.fori_loop(0,size//8,panel,0)

def frame(gram, span):
    return pl.pallas_call(
        frame_kernel,
        out_shape=jax.ShapeDtypeStruct(gram.shape,jnp.float32),
        scratch_shapes=[pltpu.VMEM(gram.shape,jnp.float32),pltpu.VMEM(gram.shape,jnp.float32)],
        compiler_params=pltpu.CompilerParams(vmem_limit_bytes=40<<20),
    )(gram,span)


def adam_update(weight, first_mom, second, gradient, step_rate):
    first_mom = BETA_ONE * first_mom + (1.0 - BETA_ONE) * gradient
    second = BETA_TWO * second + (1.0 - BETA_TWO) * gradient * gradient
    direction = (
        first_mom / (1.0 - BETA_ONE**STEP) / (jnp.sqrt(second / (1.0 - BETA_TWO**STEP)) + ADAM_EPS)
    )
    return (weight - step_rate * (direction + WEIGHT_DECAY * weight), first_mom, second)


def rotated_kernel(
    place_ref,
    factor_ref,
    weight_ref,
    first_ref,
    second_ref,
    grad_ref,
    stat_ref,
    basis_ref,
    weight_out,
    first_out,
    second_out,
    stat_out,
    gram_ref,
    span_ref,
):
    def product(left, right, dims):
        return lax.dot_general(
            left, right, (dims, ((), ())), precision=HIGHEST, preferred_element_type=jnp.float32
        )

    basis = basis_ref[0, 0]
    gradient = jnp.concatenate(
        [grad_ref[(place_ref[0] + PLANES - piece) % PLANES] for piece in range(PLANES)], 0
    )
    gradient = gradient.astype(jnp.float32) * factor_ref[0, 0]
    turned = product(gradient, basis, ((1,), (0,)))
    first_mom = BETA_ONE * first_ref[...] + (1.0 - BETA_ONE) * turned
    second = BETA_TWO * second_ref[...] + (1.0 - BETA_TWO) * turned * turned
    direction = (
        first_mom / (1.0 - BETA_ONE**STEP) / (jnp.sqrt(second / (1.0 - BETA_TWO**STEP)) + ADAM_EPS)
    )
    back = product(direction, basis, ((1,), (1,)))
    weight = weight_ref[...]
    weight_out[...] = weight - RATE_LAYER * (back + WEIGHT_DECAY * weight)
    first_out[...] = first_mom
    second_out[...] = second
    stat_next = BETA_STAT * stat_ref[0, 0] + (1.0 - BETA_STAT) * product(
        gradient, gradient, ((0,), (0,))
    )
    stat_out[0, 0] = stat_next
    spanned = product(stat_next, basis, ((1,), (0,)))
    turned_span = spanned.T
    span_ref[0] = turned_span
    gram_ref[0] = product(turned_span, spanned, ((1,), (0,)))


def rotated_update(weight, first_mom, second, gradient, factor, stat, basis):
    blocks, block_len = basis.shape[1], basis.shape[2]
    rows = weight.shape[0]
    column = pl.BlockSpec((rows, block_len), lambda b: (0, b))
    square = pl.BlockSpec((1, 1, block_len, block_len), lambda b: (0, b, 0, 0))
    flat = pl.BlockSpec((1, block_len, block_len), lambda b: (b, 0, 0))
    wide = jax.ShapeDtypeStruct(weight.shape, jnp.float32)
    small = jax.ShapeDtypeStruct((blocks, block_len, block_len), jnp.float32)
    weight_next, first_next, second_next, stat_next, gram, span = pl.pallas_call(
        rotated_kernel,
        grid=(blocks,),
        in_specs=[pl.BlockSpec(memory_space=pltpu.SMEM)] * 2
        + [column] * 3
        + [pl.BlockSpec((PLANES, rows // PLANES, block_len), lambda b: (0, 0, b))]
        + [square] * 2,
        out_specs=[column] * 3 + [square] + [flat] * 2,
        out_shape=[wide] * 3 + [jax.ShapeDtypeStruct(stat.shape, jnp.float32)] + [small] * 2,
        compiler_params=pltpu.CompilerParams(vmem_limit_bytes=40 << 20),
    )(lax.axis_index(PLANE).reshape(1), factor.reshape(1, 1), weight, first_mom, second, gradient, stat, basis)
    solved = frame(gram, span)
    return (weight_next, first_next, second_next, jnp.swapaxes(solved, 1, 2)[None], stat_next)


def body(
    token_ids,
    lengths,
    loss_place,
    targets,
    loss_flag,
    layer_weight,
    layer_first,
    layer_second,
    rot_basis,
    stat_matrix,
    small_params,
    small_first,
    small_second,
    embed_table,
    table_first,
    table_second,
):
    group_id = lax.axis_index(VOCAB)
    groups = lax.axis_size(VOCAB)
    part_count = lax.axis_size(SEQ)
    ways = lax.axis_size("w")
    at_x, at_y, at_c = (lax.axis_index(name) for name in ("x", "y", "core"))
    tok_rows = token_ids.shape[0] // groups
    loss_rows = loss_place.shape[0] // groups
    vocab_rows, slice_width = embed_table.shape
    vocab_live = min(groups * vocab_rows, VOCAB_REAL)
    model_dim = layer_weight.shape[1]
    hidden_units = small_params.shape[0] - 10 * model_dim
    head_width = model_dim // part_count
    length = part_count * tok_rows
    (
        bias_q,
        bias_v,
        bias_out,
        bias_up,
        bias_down,
        gain_one,
        shift_one,
        gain_two,
        shift_two,
        gain_final,
        shift_final,
    ) = pieces(small_params, model_dim, hidden_units)

    at_a, at_b = lax.axis_index("za"), lax.axis_index("zb")
    order = Order()
    weight_low = layer_weight.astype(jnp.bfloat16)
    gathered = lax.all_gather(weight_low, ALL, axis=0, tiled=True)
    table_low = embed_table.astype(jnp.bfloat16)
    other_low = swap(table_low, "zb")
    far_low = swap(table_low, "y")
    pair = in_order(at_b, table_low, other_low, 0)
    table_near = in_order(at_c, pair, swap(pair, "core"), 1)

    pair_rows = 2 * vocab_rows
    pair_range = jnp.arange(pair_rows, dtype=jnp.int32)
    plane_step = 2 * ways * vocab_rows
    first_start = (group_id - at_b * 2 * ways) * vocab_rows

    def in_pair(ids):
        one, two = ids - first_start, ids - first_start - plane_step
        inside = (one >= 0) & (one < vocab_rows)
        both = (two >= 0) & (two < vocab_rows)
        return jnp.where(inside, one, jnp.where(both, two + vocab_rows, -1))

    def of_this_b(tensor):
        shaped = pick(tensor.reshape(2, 2, ways, 2, -1, tensor.shape[-1]), at_b, 1)
        return own_first(own_first(shaped, at_a, 0), at_x, 2)

    own_ids = of_this_b(token_ids)
    near_ids = in_order(at_c, own_ids, swap(own_ids, "core"), 4)
    all_ids = in_order(at_y, near_ids, swap(near_ids, "y"), 4).swapaxes(3, 4)

    def looked_up(ids, rows_of):
        hot = (in_pair(ids).reshape(-1, 1) == pair_range[None, :]).astype(jnp.bfloat16)
        got = plain_dot(hot, rows_of).astype(jnp.bfloat16)
        return got.reshape(2, ways, tok_rows, -1)

    near = [looked_up(own_ids[at], table_near) for at in (1, 0)]
    far_low = order.hold(far_low, near[0])
    far_other = order.hold(swap(other_low, "y"), near[1])
    pair = in_order(at_b, far_low, far_other, 0)
    table_far = in_order(at_c, pair, swap(pair, "core"), 1)
    far = [looked_up(own_ids[at], table_far) for at in (1, 0)]
    half_near = to_group(*near)
    half_far = to_group(*far)
    embedded = in_order(at_y, half_near, half_far, 1)
    table_full = in_order(at_y, table_near, table_far, 1)

    group_lengths = jnp.take(lengths, group_id, axis=0)
    bounds = jnp.cumsum(group_lengths)[:-1]
    positions = jnp.arange(length, dtype=jnp.int32)
    starts = jnp.max(
        jnp.where(positions[:, None] >= bounds[None, :], bounds[None, :], 0), 1
    ).astype(jnp.int32)[None]

    normed_low = layer_norm(embedded, gain_one, shift_one).astype(jnp.bfloat16)
    joined = low_dot(normed_low, gathered[: 3 * model_dim]) + jnp.concatenate(
        [bias_q, jnp.zeros_like(bias_q), bias_v]
    )
    joined_heads = lax.all_to_all(
        joined.astype(jnp.bfloat16).reshape(tok_rows, 3, part_count, head_width),
        SEQ,
        split_axis=2,
        concat_axis=0,
        tiled=True,
    )
    queries, key_rows, values = (joined_heads[:, at, 0] for at in range(3))
    mixture, mixture_wide, logsum = attend(starts, queries, key_rows, values)
    mixed_low = lax.all_to_all(
        mixture.reshape(part_count, tok_rows, 1, head_width),
        SEQ,
        split_axis=0,
        concat_axis=2,
        tiled=True,
    ).reshape(tok_rows, model_dim)
    project_out = gathered[3 * model_dim : 4 * model_dim]
    expand_weight = gathered[4 * model_dim : 4 * model_dim + hidden_units]
    reduce_weight = gathered[4 * model_dim + hidden_units :]
    middle = embedded + low_dot(mixed_low, project_out) + bias_out
    normed_two_low = layer_norm(middle, gain_two, shift_two).astype(jnp.bfloat16)
    hidden = low_dot(normed_two_low, expand_weight) + bias_up
    active_low = smooth(hidden).astype(jnp.bfloat16)
    residual_out = middle + plain_dot(active_low, reduce_weight) + bias_down
    final_out = layer_norm(residual_out, gain_final, shift_final)
    own_pos = lax.dynamic_slice_in_dim(loss_place[:, 0], group_id * loss_rows, loss_rows, 0)
    pos_hot = own_pos[:, None] == jnp.arange(tok_rows, dtype=jnp.int32)[None, :]
    chosen = plain_dot(pos_hot.astype(jnp.bfloat16), final_out.astype(jnp.bfloat16)).astype(
        jnp.bfloat16
    )

    head_rows = from_groups(chosen).reshape(-1, model_dim)
    logits = low_dot(head_rows, table_full)
    if groups * vocab_rows > vocab_live:
        live = jnp.minimum(vocab_live - first_start, vocab_rows)
        live_two = vocab_live - first_start - plane_step
        kept = jnp.where(pair_range < vocab_rows, pair_range < live, pair_range - vocab_rows < live_two)
        logits = jnp.where(kept[None, :], logits, MASKED)
    target_hot = pair_range[None, :] == in_pair(of_this_b(targets)).reshape(-1, 1)
    target_part = jnp.sum(jnp.where(target_hot, logits, 0.0), 1)
    local_peak = jnp.max(logits, 1)
    local_sum = jnp.sum(jnp.exp(logits - local_peak[:, None]), 1)
    everyone = from_groups(jnp.stack([local_peak, local_sum, target_part]))
    everyone = everyone.reshape(2, 2, ways, 3, 2, 2, -1)
    aligned = []
    for by_x in (0, 1):
        for by_a in (0, 1):
            turned = jnp.roll(everyone[by_x, by_a], (by_x, by_a), (2, 3))
            aligned.append(turned.reshape(ways, 3, -1))
    everyone = jnp.concatenate(aligned, 0)
    peak_all = jnp.max(everyone[:, 0], 0)
    sum_all = jnp.sum(everyone[:, 1] * jnp.exp(everyone[:, 0] - peak_all[None]), 0)
    target_logit = jnp.sum(everyone[:, 2], 0)
    logsum_all = peak_all + jnp.log(sum_all)
    weight_rows = of_this_b(loss_flag).reshape(-1).astype(jnp.float32)
    chance = jnp.exp(logits - logsum_all[:, None])
    grad_logits = weight_rows[:, None] * (chance - target_hot.astype(jnp.float32))
    grad_low = grad_logits.astype(jnp.bfloat16)
    grad_rows = plain_dot(grad_low, table_full).astype(jnp.bfloat16)
    grad_rows = grad_rows.reshape(2, 2, ways, loss_rows, model_dim)
    grad_chosen = to_group(grad_rows[1], grad_rows[0])

    def table_part(by_y, by_c):
        place = (at_y ^ by_y) * 2 + (at_c ^ by_c)
        cols = lax.dynamic_slice_in_dim(head_rows, place * slice_width, slice_width, 1)
        return outer_dot(grad_low, cols).astype(jnp.bfloat16)

    far_sum = lowered(table_part(1, 0), swap(table_part(1, 1), "core"))
    near_sum = added(table_part(0, 0), swap(table_part(0, 1), "core"))
    grad_chosen = order.hold(grad_chosen, near_sum, far_sum, all_ids)
    head_table_grad = added(near_sum, swap(far_sum, "y"))

    grad_final = lax.dot_general(
        pos_hot.astype(jnp.float32),
        grad_chosen,
        (((0,), (0,)), ((), ())),
        precision=HIGHEST,
        preferred_element_type=jnp.float32,
    )

    is_first = group_id == 2 * ways * at_b
    loss_part = jnp.where(is_first, jnp.sum(weight_rows * (logsum_all - target_logit)), 0.0)
    count_part = jnp.where(is_first, jnp.sum(weight_rows), 0.0)
    unused, final_back = jax.vjp(layer_norm, residual_out, gain_final, shift_final)
    grad_resid, grad_gain_final, grad_shift_final = final_back(grad_final)
    resid_low = grad_resid.astype(jnp.bfloat16)
    grad_bias_down = column_sum(resid_low)
    plane_rows = layer_weight.shape[0] * groups * part_count // PLANES
    reduce_cut = hidden_units - plane_rows
    plane_three = outer_dot(active_low[:, reduce_cut:], resid_low, jnp.bfloat16)
    piece_three = reduce_plane(plane_three)
    resid_low = order.hold(resid_low, plane_three)
    grad_active = low_dot(resid_low, reduce_weight)
    unused, gelu_back = jax.vjp(smooth, hidden)
    hidden_low = gelu_back(grad_active)[0].astype(jnp.bfloat16)
    grad_bias_up = column_sum(hidden_low)
    half = plane_rows - model_dim
    plane_two = jnp.concatenate(
        [
            outer_dot(hidden_low[:, half:], normed_two_low, jnp.bfloat16),
            outer_dot(active_low[:, :reduce_cut], resid_low, jnp.bfloat16),
        ],
        0,
    )
    piece_two = reduce_plane(plane_two)
    unused, two_back = jax.vjp(layer_norm, middle, gain_two, shift_two)
    grad_middle_part, grad_gain_two, grad_shift_two = two_back(plain_dot(hidden_low, expand_weight))
    grad_middle = grad_resid + grad_middle_part
    middle_low = grad_middle.astype(jnp.bfloat16)
    grad_bias_out = column_sum(middle_low)
    grad_mixed = plain_dot(middle_low, project_out)
    grad_heads = lax.all_to_all(
        grad_mixed.astype(jnp.bfloat16).reshape(tok_rows, part_count, head_width),
        SEQ,
        split_axis=1,
        concat_axis=0,
        tiled=True,
    )[:, 0]
    core_one = scatter_core(
        jnp.concatenate(
            [
                outer_dot(middle_low, mixed_low, jnp.bfloat16),
                outer_dot(hidden_low[:, :half], normed_two_low, jnp.bfloat16),
            ],
            0,
        )
    )
    grad_heads = order.hold(grad_heads, plane_two)
    grad_query, grad_keys, grad_values = attend_back(
        starts, queries, key_rows, values, grad_heads, mixture_wide, logsum
    )
    grad_heads = order.hold(jnp.stack([grad_query, grad_keys, grad_values], 1), core_one)
    grad_joined = lax.all_to_all(
        grad_heads.reshape(part_count, tok_rows, 3, 1, head_width),
        SEQ,
        split_axis=0,
        concat_axis=3,
        tiled=True,
    ).reshape(tok_rows, 3 * model_dim)
    core_zero = scatter_core(outer_dot(grad_joined, normed_low, jnp.bfloat16))
    unused, one_back = jax.vjp(layer_norm, embedded, gain_one, shift_one)
    grad_embed_part, grad_gain_one, grad_shift_one = one_back(plain_dot(grad_joined, gathered[: 3 * model_dim]))
    rows_back = (grad_middle + grad_embed_part).astype(jnp.bfloat16)
    first_one = scatter_first(order.hold(core_one, grad_joined))
    rows_back = order.hold(rows_back, core_zero)
    rows_back = lax.all_to_all(rows_back, SEQ, split_axis=1, concat_axis=0, tiled=True)
    grad_bias_q = column_sum(grad_joined[:, :model_dim])
    grad_bias_v = column_sum(grad_joined[:, 2 * model_dim :])
    first_zero = scatter_first(core_zero)
    second_one = scatter_second(first_one)
    second_zero = scatter_second(first_zero)
    row_range = jnp.arange(vocab_rows, dtype=jnp.int32)[:, None]
    sides = {"mine": at_b, "theirs": 1 - at_b}
    spread = {
        name: lax.dynamic_slice_in_dim(head_table_grad, side * vocab_rows, vocab_rows, 0)
        for name, side in sides.items()
    }
    rows_back = rows_back.reshape(2, length // 2, slice_width)
    id_halves = all_ids.reshape(2, 2, ways, 2, length // 2)
    for at in range(2):
        got = from_groups(rows_back[at], order, (first_one, first_zero)[at])
        got = order.hold(got, (second_one, second_zero)[at]).reshape(-1, slice_width)
        ids = id_halves[:, :, :, at].reshape(1, -1) - first_start
        for name, side in sides.items():
            hot = (row_range == ids - side * plane_step).astype(jnp.bfloat16)
            spread[name] = spread[name] + plain_dot(hot, got)
    table_grad = added(spread["mine"], swap(spread["theirs"].astype(jnp.bfloat16), "zb"))
    piece_one = scatter_last(second_one)
    piece_zero = scatter_last(second_zero)
    quarters = jnp.stack([piece_zero, piece_one, piece_two, piece_three])
    layer_grad = jnp.stack(sent_z([pick(quarters, plane) for plane in planes_from_here()]))
    squares = jnp.sum(jnp.square(layer_grad.astype(jnp.float32))) + jnp.sum(
        table_grad * table_grad
    )
    totals = total_of(
        jnp.concatenate(
            [
                grad_bias_q,
                grad_bias_v,
                grad_bias_out,
                grad_bias_up,
                grad_bias_down,
                grad_gain_one,
                grad_shift_one,
                grad_gain_two,
                grad_shift_two,
                grad_gain_final,
                grad_shift_final,
                jnp.stack([squares, loss_part, count_part]),
            ]
        )
    )
    squares, loss_sum, loss_count = totals[-3], totals[-2], totals[-1] + order.zero()
    small_grad = totals[:-3]
    gradient_norm = jnp.sqrt(squares + jnp.sum(small_grad * small_grad))
    factor = 1.0 / jnp.maximum(gradient_norm, 1.0)
    out_bias_grad = factor * small_grad[2 * model_dim : 3 * model_dim]
    layer_next, layer_first_next, layer_second_next, basis_next, stat_next = rotated_update(
        layer_weight, layer_first, layer_second, layer_grad, factor, stat_matrix, rot_basis
    )
    small_next, small_first_next, small_second_next = adam_update(
        small_params, small_first, small_second, factor * small_grad, RATE_SMALL
    )
    table_next, table_first_next, table_second_next = adam_update(
        embed_table, table_first, table_second, factor * table_grad, RATE_TABLE
    )
    return (
        loss_sum,
        loss_count,
        gradient_norm,
        layer_next,
        layer_first_next,
        layer_second_next,
        basis_next,
        stat_next,
        small_next,
        small_first_next,
        small_second_next,
        table_next,
        table_first_next,
        table_second_next,
        out_bias_grad,
    )


def solution(mesh):
    vocab, seq = mesh.shape["vocab"], mesh.shape["seq"]
    inner = Mesh(mesh.devices.reshape(2, 2, vocab // 8, 2, seq // 2, 2), ALL)
    in_specs = (
        P(None, SEQ),
        P(),
        P(None, SEQ),
        P(None, SEQ),
        P(None, SEQ),
        P(ALL, None),
        P(ALL, None),
        P(ALL, None),
        P(ALL, None, None, None),
        P(ALL, None, None, None),
        P(),
        P(),
        P(),
        P(VOCAB, SEQ),
        P(VOCAB, SEQ),
        P(VOCAB, SEQ),
    )
    out_specs = (
        P(),
        P(),
        P(),
        P(ALL, None),
        P(ALL, None),
        P(ALL, None),
        P(ALL, None, None, None),
        P(ALL, None, None, None),
        P(),
        P(),
        P(),
        P(VOCAB, SEQ),
        P(VOCAB, SEQ),
        P(VOCAB, SEQ),
        P(),
    )
    return jax.shard_map(body, mesh=inner, in_specs=in_specs, out_specs=out_specs, check_vma=False)
```

```python
from functools import partial

import jax
import jax.numpy as jnp
from jax import lax
from jax.experimental import pallas as pl
from jax.experimental.pallas import tpu as pltpu
from jax.sharding import Mesh, PartitionSpec as P

HEAD_SIZE = 64
VOCAB_REAL = 50257
STEP = 5


NORM_EPS = 1e-05
BETA_ONE = 0.9
BETA_TWO = 0.95
BETA_STAT = 0.95
ADAM_EPS = 1e-08
WEIGHT_DECAY = 0.1
RATE_LAYER = 0.025
RATE_SMALL = 0.08
RATE_TABLE = 0.04
MASKED = -1e30
HIGHEST = lax.Precision.HIGHEST
LANES_BOTH = (((1,), (1,)), ((), ()))
PLANE = ("za", "zb")
VOCAB = PLANE + ("w", "x")
SEQ = ("y", "core")
ALL = VOCAB + SEQ
OWNERS = ("w", "x", "y", "core")
PLANES = 4


def layer_norm(inputs, gain, shift):
    centre = inputs - jnp.mean(inputs, -1, keepdims=True)
    spread = jnp.mean(centre * centre, -1, keepdims=True)
    return centre * lax.rsqrt(spread + NORM_EPS) * (1.0 + gain) + shift


def smooth(inputs):
    return jax.nn.gelu(inputs, approximate=True)


def low_dot(left, right):
    return lax.dot_general(left, right, LANES_BOTH, preferred_element_type=jnp.float32)


def plain_dot(left, right):
    return jnp.dot(left, right, preferred_element_type=jnp.float32)


def outer_dot(left, right, kind=jnp.float32):
    return lax.dot_general(left, right, (((0,), (0,)), ((), ())), preferred_element_type=kind)


def column_sum(values):
    return jnp.sum(values.astype(jnp.float32), 0)


def pieces(small_params, model_dim, hidden_units):
    bounds = [0, model_dim, 2 * model_dim, 3 * model_dim, 3 * model_dim + hidden_units]
    for place_id in range(7):
        bounds.append(bounds[-1] + model_dim)
    return [small_params[bounds[place_id] : bounds[place_id + 1]] for place_id in range(11)]


def swap(tensor, axis):
    return lax.ppermute(tensor, axis, [(0, 1), (1, 0)])


def shift(tensor, step):
    step %= PLANES
    if step == 0:
        return tensor
    return lax.ppermute(tensor, PLANE, [(i, (i + step) % PLANES) for i in range(PLANES)])


def planes_from_here():
    return [(lax.axis_index(PLANE) + step) % PLANES for step in range(PLANES)]


def gathered_z(tensor):
    return [shift(tensor, -step) for step in range(PLANES)]


def sent_z(terms):
    return [shift(terms[step], step) for step in range(PLANES)]


def pick(tensor, place, axis=0):
    return lax.dynamic_index_in_dim(tensor, place, axis, keepdims=False)


def added(*tensors):
    total = tensors[0].astype(jnp.float32)
    for tensor in tensors[1:]:
        total = total + tensor.astype(jnp.float32)
    return total


def lowered(*tensors):
    return added(*tensors).astype(jnp.bfloat16)


def in_order(place, own, other, axis):
    return jnp.where(
        place == 0, jnp.concatenate([own, other], axis), jnp.concatenate([other, own], axis)
    )


class Order:
    def __init__(self):
        self.marks = []

    def hold(self, tensors, *earlier):
        marks = [lax.slice(t, (0,) * t.ndim, (1,) * t.ndim).reshape(()) for t in earlier]
        tensors, *marks = lax.optimization_barrier((tensors, *marks))
        self.marks += [mark.astype(jnp.float32) for mark in marks]
        return tensors

    def zero(self):
        return sum(0.0 * mark for mark in self.marks)


def flip(tensor, by_core):
    pairs = []
    for place in range(8):
        pairs.append((place, place ^ (4 if by_core[place % 2] == "x" else 2)))
    return lax.ppermute(tensor, ("x", "y", "core"), pairs)


def by_owner(grads, planes):
    shape = (planes, lax.axis_size(ALL), -1, grads.shape[1])
    return lax.optimization_barrier(grads.reshape(shape))


def reduce_planes(grads):
    return lax.psum_scatter(grads, OWNERS + PLANE, scatter_dimension=1, tiled=False)


def as_is(tensor):
    return tensor


def scatter_core(grads, wait=as_is):
    model_dim = grads.shape[1]
    at_c = lax.axis_index("core")
    shaped = grads.reshape(lax.axis_size("w"), 2, 2, 2, -1, model_dim)
    return lowered(pick(shaped, at_c, 3), wait(swap(pick(shaped, 1 - at_c, 3), "core")))


def scatter_first(shaped, wait=as_is):
    at_x, at_y, at_c = (lax.axis_index(name) for name in ("x", "y", "core"))
    ways, unused, unused, rows, model_dim = shaped.shape
    shaped = shaped.reshape(ways, 4, rows, model_dim)

    def half(x, y):
        spots = (jnp.where(at_c == 0, y, 2 * x), jnp.where(at_c == 0, 2 + y, 2 * x + 1))
        return jnp.stack([pick(shaped, spot, 1) for spot in spots], 1)

    return lowered(half(at_x, at_y), wait(flip(half(1 - at_x, 1 - at_y), "yx")))


def scatter_second(pair, wait=as_is):
    spot = jnp.where(lax.axis_index("core") == 0, lax.axis_index("x"), lax.axis_index("y"))
    own = lowered(pick(pair, spot, 1), wait(flip(pick(pair, 1 - spot, 1), "xy")))
    if lax.axis_size("w") > 1:
        own = lax.psum_scatter(own, "w", scatter_dimension=0, tiled=True)
    return own[0]


def scatter_last(own, wait=as_is):
    rows, model_dim = own.shape
    quarters = own.reshape(PLANES, rows // PLANES, model_dim)
    got = sent_z([pick(quarters, plane) for plane in planes_from_here()])
    return lowered(got[0], *[wait(part) for part in got[1:]])


def own_first(tensor, place, axis):
    return jnp.stack([pick(tensor, place, axis), pick(tensor, 1 - place, axis)])


def over_x(theirs, mine):
    both = lowered(mine, swap(theirs, "x"))
    if lax.axis_size("w") > 1:
        return lax.psum_scatter(both, "w", scatter_dimension=1, tiled=False)
    return both[:, 0]


def from_groups(tensor, wait=as_is):
    if lax.axis_size("w") > 1:
        tensor = lax.all_gather(tensor, "w", axis=0, tiled=False)
    else:
        tensor = tensor[None]
    both = [tensor, wait(swap(tensor, "za"))]
    return jnp.stack(both + [swap(part, "x") for part in both]).reshape((2, 2) + tensor.shape)


def total_of(values):
    for name in ("core", "y", "x", "zb", "za"):
        values = values + swap(values, name)
    return lax.psum(values, "w") if lax.axis_size("w") > 1 else values


def total_at_once(value):
    spread = jnp.broadcast_to(value, (lax.axis_size(ALL), 1))
    return jnp.sum(lax.all_to_all(spread, ALL, split_axis=0, concat_axis=0, tiled=True))


def _groups(width):
    return [(at,min(128,width-at)) for at in range(0,width,128)]

def _head_part(rows, at, wide):
    lane=lax.broadcasted_iota(jnp.int32,rows.shape,1)
    return jnp.where((lane>=at)&(lane<at+wide),rows,jnp.zeros_like(rows))

def attend_kernel(start_ref, q_ref, k_ref, v_ref, low_ref, out_ref, lse_ref, vt_ref):
    block=q_ref.shape[2]
    step=pl.program_id(0)
    width=q_ref.shape[3]
    for at,wide in _groups(width):
        @pl.when(step==0)
        def _():
            for part in range(v_ref.shape[0]):
                vt_ref[part,at:at+wide,:]=v_ref[part,0,:,at:at+wide].astype(jnp.float32).T.astype(jnp.bfloat16)
    start=start_ref[...]
    sub=lax.broadcasted_iota(jnp.int32,(block,block),0)
    lane=lax.broadcasted_iota(jnp.int32,(block,block),1)
    groups=_groups(width)
    heads=[(at,h) for at,wide in groups for h in range(wide//HEAD_SIZE)]
    parts=[]
    for at,wide in groups:
        queries=q_ref[0,0,:,at:at+wide]*jnp.bfloat16(HEAD_SIZE**-0.5)
        parts+=[_head_part(queries,h*HEAD_SIZE,HEAD_SIZE) for h in range(wide//HEAD_SIZE)]
    def chunk(place, carry, diag):
        offset=place*block
        allowed=sub>=start-offset
        if diag:
            allowed=allowed&(sub<=lane)
        fresh=[]
        scored=[]
        for i,(at,h) in enumerate(heads):
            keys=k_ref[place,0,:,at:min(at+128,width)]
            scores=lax.dot_general(keys,parts[i],LANES_BOTH,preferred_element_type=jnp.float32)
            scored.append(jnp.where(allowed,scores,MASKED))
        for i,(at,h) in enumerate(heads):
            peak,total,acc=carry[i]
            scores=scored[i]
            higher=jnp.maximum(peak,jnp.max(scores,0,keepdims=True))
            raised=jnp.exp(scores-higher)
            shrink=jnp.exp(peak-higher)
            vt=vt_ref[place,i*HEAD_SIZE:(i+1)*HEAD_SIZE,:]
            acc=acc*shrink+jnp.dot(vt,raised.astype(jnp.bfloat16),preferred_element_type=jnp.float32)
            fresh.append((higher,total*shrink+jnp.sum(raised,0,keepdims=True),acc))
        return tuple(fresh)
    carry=tuple((jnp.full((1,block),MASKED,jnp.float32),jnp.zeros((1,block),jnp.float32),jnp.zeros((HEAD_SIZE,block),jnp.float32)) for h in heads)
    carry=lax.fori_loop(0,step,lambda c,x:chunk(c,x,False),carry)
    carry=chunk(step,carry,True)
    for at,wide in groups:
        own=carry[at//HEAD_SIZE:(at+wide)//HEAD_SIZE]
        mixed=jnp.concatenate([acc*(1.0/total) for peak,total,acc in own],0).T
        out_ref[0,:,at:at+wide]=mixed
        low_ref[0,:,at:at+wide]=mixed.astype(jnp.bfloat16)
    for i in range(len(heads)):
        peak,total,acc=carry[i]
        lse_ref[i:i+1,:]=peak+jnp.log(total)

def attend(start, joined):
    parts,_,block,width=joined.shape
    length=parts*block
    rows=lambda i:(i,0,0)
    cols=lambda i:(0,i)
    one=pl.BlockSpec((1,1,block,width),lambda i:(i,0,0,0))
    every=[pl.BlockSpec((parts,1,block,width),lambda i,at=at:(0,at,0,0)) for at in (1,2)]
    return pl.pallas_call(
        attend_kernel,
        grid=(parts,),
        in_specs=[pl.BlockSpec((1,block),cols),one]+every,
        out_specs=[pl.BlockSpec((1,block,width),rows),pl.BlockSpec((1,block,width),rows),pl.BlockSpec((8,block),cols)],
        out_shape=[jax.ShapeDtypeStruct((parts,block,width),jnp.bfloat16),jax.ShapeDtypeStruct((parts,block,width),jnp.float32),jax.ShapeDtypeStruct((8,length),jnp.float32)],
        scratch_shapes=[pltpu.VMEM((parts,width,block),jnp.bfloat16)],
        compiler_params=pltpu.CompilerParams(vmem_limit_bytes=40<<20,dimension_semantics=("arbitrary",)),
    )(start,joined,joined,joined)

def attend_back_kernel(start_ref, q_ref, k_ref, v_ref, do_ref, out_ref, lse_ref, grad_ref, kt_ref, dka_ref, dva_ref):
    block=q_ref.shape[2]
    step=pl.program_id(0)
    width=q_ref.shape[3]
    @pl.when(step==0)
    def _():
        for at,wide in _groups(width):
            for part in range(k_ref.shape[0]):
                kt_ref[part,at:at+wide,:]=k_ref[part,0,:,at:at+wide].astype(jnp.float32).T.astype(jnp.bfloat16)
        dka_ref[...]=jnp.zeros_like(dka_ref)
        dva_ref[...]=jnp.zeros_like(dva_ref)
    start=start_ref[...]
    sub=lax.broadcasted_iota(jnp.int32,(block,block),0)
    lane=lax.broadcasted_iota(jnp.int32,(block,block),1)
    temper=HEAD_SIZE**-0.5
    for at,wide in _groups(width):
        queries=q_ref[0,0,:,at:at+wide]*jnp.bfloat16(temper)
        grads=do_ref[0,:,at:at+wide]
        heads=range(wide//HEAD_SIZE)
        parts=[_head_part(queries,h*HEAD_SIZE,HEAD_SIZE) for h in heads]
        dparts=[_head_part(grads,h*HEAD_SIZE,HEAD_SIZE) for h in heads]
        crossed=(grads.astype(jnp.float32)*out_ref[0,:,at:at+wide]).T
        deltas=[jnp.sum(crossed[h*HEAD_SIZE:(h+1)*HEAD_SIZE],0,keepdims=True) for h in heads]
        lses=[lse_ref[at//HEAD_SIZE+h:at//HEAD_SIZE+h+1,:] for h in heads]
        def chunk(place, carry, diag):
            offset=place*block
            keys=k_ref[place,0,:,at:at+wide]
            values=v_ref[place,0,:,at:at+wide]
            allowed=sub>=start-offset
            if diag:
                allowed=allowed&(sub<=lane)
            fresh=[]
            dkey=None
            for h in heads:
                scores=lax.dot_general(keys,parts[h],LANES_BOTH,preferred_element_type=jnp.float32)
                chance=jnp.exp(jnp.where(allowed,scores,MASKED)-lses[h])
                dchance=lax.dot_general(values,dparts[h],LANES_BOTH,preferred_element_type=jnp.float32)
                dscores=(chance*(dchance-deltas[h])).astype(jnp.bfloat16)
                one=jnp.dot(dscores,parts[h],preferred_element_type=jnp.float32)
                two=jnp.dot(chance.astype(jnp.bfloat16),dparts[h],preferred_element_type=jnp.float32)
                dkey,dval=(one,two) if dkey is None else (dkey+one,dval+two)
                kt=kt_ref[place,at+h*HEAD_SIZE:at+(h+1)*HEAD_SIZE,:]
                fresh.append(carry[h]+jnp.dot(kt,dscores,preferred_element_type=jnp.float32))
            dka_ref[place,:,at:at+wide]+=dkey
            dva_ref[place,:,at:at+wide]+=dval
            return tuple(fresh)
        carry=tuple(jnp.zeros((HEAD_SIZE,block),jnp.float32) for h in heads)
        carry=lax.fori_loop(0,step,lambda c,x:chunk(c,x,False),carry)
        carry=chunk(step,carry,True)
        grad_ref[step,0,:,at:at+wide]=(jnp.concatenate(carry,0).T*temper).astype(jnp.bfloat16)
    @pl.when(step==pl.num_programs(0)-1)
    def _():
        grad_ref[:,1]=dka_ref[...].astype(jnp.bfloat16)
        grad_ref[:,2]=dva_ref[...].astype(jnp.bfloat16)

def attend_back(start, joined, grad, out, lse):
    parts,_,block,width=joined.shape
    rows=lambda i:(i,0,0)
    cols=lambda i:(0,i)
    one=pl.BlockSpec((1,1,block,width),lambda i:(i,0,0,0))
    every=[pl.BlockSpec((parts,1,block,width),lambda i,at=at:(0,at,0,0)) for at in (1,2)]
    return pl.pallas_call(
        attend_back_kernel,
        grid=(parts,),
        in_specs=[pl.BlockSpec((1,block),cols),one]+every+[pl.BlockSpec((1,block,width),rows),pl.BlockSpec((1,block,width),rows),pl.BlockSpec((8,block),cols)],
        out_specs=pl.BlockSpec(joined.shape,lambda i:(0,0,0,0)),
        out_shape=jax.ShapeDtypeStruct(joined.shape,jnp.bfloat16),
        scratch_shapes=[pltpu.VMEM((parts,width,block),jnp.bfloat16),pltpu.VMEM((parts,block,width),jnp.float32),pltpu.VMEM((parts,block,width),jnp.float32)],
        compiler_params=pltpu.CompilerParams(vmem_limit_bytes=40<<20,dimension_semantics=("arbitrary",)),
    )(start,joined,joined,joined,grad,out,lse)


def join_kernel(rows_ref, weight_ref, bias_ref, out_ref):
    width=out_ref.shape[3]
    joined=lax.dot_general(rows_ref[...],weight_ref[...],LANES_BOTH,preferred_element_type=jnp.float32)
    joined=(joined+bias_ref[...]).astype(jnp.bfloat16)
    for place in range(out_ref.shape[0]):
        out_ref[place,0]=joined[:,place*width:(place+1)*width]


def join(rows, weights, bias, parts):
    count,model_dim=rows.shape
    width=model_dim//parts
    pairs=parts//2
    return pl.pallas_call(
        join_kernel,
        grid=(3,pairs),
        in_specs=[pl.BlockSpec((count,model_dim),lambda p,h:(0,0)),
                  pl.BlockSpec((2*width,model_dim),lambda p,h:(p*pairs+h,0)),
                  pl.BlockSpec((1,2*width),lambda p,h:(0,p*pairs+h))],
        out_specs=pl.BlockSpec((2,1,count,width),lambda p,h:(h,p,0,0)),
        out_shape=jax.ShapeDtypeStruct((parts,3,count,width),jnp.bfloat16),
        compiler_params=pltpu.CompilerParams(vmem_limit_bytes=40<<20,dimension_semantics=("arbitrary","arbitrary")),
    )(rows,weights,bias)


def frame_kernel(gram_ref, span_ref, out_ref, work_ref):
    count,size,_=gram_ref.shape
    work_ref[...]=gram_ref[...]
    out_ref[...]=span_ref[...]
    rows=lax.broadcasted_iota(jnp.int32,(size,size),0)
    sub=lax.broadcasted_iota(jnp.int32,(count,32,size),1)
    def panel(step, unused):
        top=pl.multiple_of(step*32,32)
        left=work_ref[:,pl.ds(top,32),:].reshape(count*32,size)
        left=pltpu.roll(left,(size-top)%size,1).reshape(count,32,size)
        right=out_ref[:,pl.ds(top,32),:]
        for k in range(32):
            column=left[:,:,k:k+1]
            pivot=column[:,k:k+1,:]
            inverse=lax.rsqrt(pivot)
            inverse=inverse*(1.5-0.5*pivot*inverse*inverse)
            row_left=left[:,k:k+1,:]*inverse
            row_right=right[:,k:k+1,:]*inverse
            share=jnp.where(sub>k,column*inverse,0.0)
            left=jnp.where(sub==k,row_left,left-share*row_left)
            right=jnp.where(sub==k,row_right,right-share*row_right)
        out_ref[:,pl.ds(top,32),:]=right
        left=pltpu.roll(left.reshape(count*32,size),top,1).reshape(count,32,size)
        below=rows>=top+32
        @pl.when(step<size//32-1)
        def _():
            for b in range(count):
                for ref,part in ((work_ref,left[b]),(out_ref,right[b])):
                    change=lax.dot_general(left[b],part,(((0,),(0,)),((),())),precision=lax.Precision.HIGHEST,preferred_element_type=jnp.float32)
                    ref[b]=jnp.where(below,ref[b]-change,ref[b])
        return unused
    lax.fori_loop(0,size//32,panel,0)

def frame(gram, span):
    return pl.pallas_call(
        frame_kernel,
        out_shape=jax.ShapeDtypeStruct(gram.shape,jnp.float32),
        scratch_shapes=[pltpu.VMEM(gram.shape,jnp.float32)],
        compiler_params=pltpu.CompilerParams(vmem_limit_bytes=40<<20),
    )(gram,span)


def adam_update(weight, first_mom, second, gradient, step_rate):
    first_mom = BETA_ONE * first_mom + (1.0 - BETA_ONE) * gradient
    second = BETA_TWO * second + (1.0 - BETA_TWO) * gradient * gradient
    direction = (
        first_mom / (1.0 - BETA_ONE**STEP) / (jnp.sqrt(second / (1.0 - BETA_TWO**STEP)) + ADAM_EPS)
    )
    return (weight - step_rate * (direction + WEIGHT_DECAY * weight), first_mom, second)


def rotated_kernel(
    place_ref,
    factor_ref,
    weight_ref,
    first_ref,
    second_ref,
    grad_ref,
    stat_ref,
    basis_ref,
    weight_out,
    first_out,
    second_out,
    stat_out,
    gram_ref,
    span_ref,
):
    def product(left, right, dims):
        return lax.dot_general(
            left, right, (dims, ((), ())), precision=HIGHEST, preferred_element_type=jnp.float32
        )

    basis = basis_ref[0, 0]
    gradient = jnp.concatenate(
        [grad_ref[(place_ref[0] + PLANES - piece) % PLANES] for piece in range(PLANES)], 0
    )
    gradient = gradient.astype(jnp.float32) * factor_ref[0, 0]
    turned = product(gradient, basis, ((1,), (0,)))
    first_mom = BETA_ONE * first_ref[...] + (1.0 - BETA_ONE) * turned
    second = BETA_TWO * second_ref[...] + (1.0 - BETA_TWO) * turned * turned
    direction = (
        first_mom / (1.0 - BETA_ONE**STEP) / (jnp.sqrt(second / (1.0 - BETA_TWO**STEP)) + ADAM_EPS)
    )
    back = product(direction, basis, ((1,), (1,)))
    weight = weight_ref[...]
    weight_out[...] = weight - RATE_LAYER * (back + WEIGHT_DECAY * weight)
    first_out[...] = first_mom
    second_out[...] = second
    stat_next = BETA_STAT * stat_ref[0, 0] + (1.0 - BETA_STAT) * product(
        gradient, gradient, ((0,), (0,))
    )
    stat_out[0, 0] = stat_next
    spanned = product(stat_next, basis, ((1,), (0,)))
    turned_span = spanned.T
    span_ref[0] = turned_span
    gram_ref[0] = product(turned_span, spanned, ((1,), (0,)))


def rotated_update(weight, first_mom, second, gradient, factor, stat, basis):
    blocks, block_len = basis.shape[1], basis.shape[2]
    rows = weight.shape[0]
    column = pl.BlockSpec((rows, block_len), lambda b: (0, b))
    square = pl.BlockSpec((1, 1, block_len, block_len), lambda b: (0, b, 0, 0))
    flat = pl.BlockSpec((1, block_len, block_len), lambda b: (b, 0, 0))
    wide = jax.ShapeDtypeStruct(weight.shape, jnp.float32)
    small = jax.ShapeDtypeStruct((blocks, block_len, block_len), jnp.float32)
    weight_next, first_next, second_next, stat_next, gram, span = pl.pallas_call(
        rotated_kernel,
        grid=(blocks,),
        in_specs=[pl.BlockSpec(memory_space=pltpu.SMEM)] * 2
        + [column] * 3
        + [pl.BlockSpec((PLANES, rows // PLANES, block_len), lambda b: (0, 0, b))]
        + [square] * 2,
        out_specs=[column] * 3 + [square] + [flat] * 2,
        out_shape=[wide] * 3 + [jax.ShapeDtypeStruct(stat.shape, jnp.float32)] + [small] * 2,
        compiler_params=pltpu.CompilerParams(vmem_limit_bytes=40 << 20),
    )(lax.axis_index(PLANE).reshape(1), factor.reshape(1, 1), weight, first_mom, second, gradient, stat, basis)
    solved = frame(gram, span)
    return (weight_next, first_next, second_next, jnp.swapaxes(solved, 1, 2)[None], stat_next)


def body(
    token_ids,
    lengths,
    loss_place,
    targets,
    loss_flag,
    layer_weight,
    layer_first,
    layer_second,
    rot_basis,
    stat_matrix,
    small_params,
    small_first,
    small_second,
    embed_table,
    table_first,
    table_second,
):
    group_id = lax.axis_index(VOCAB)
    groups = lax.axis_size(VOCAB)
    part_count = lax.axis_size(SEQ)
    ways = lax.axis_size("w")
    at_x, at_y, at_c = (lax.axis_index(name) for name in ("x", "y", "core"))
    tok_rows = token_ids.shape[0] // groups
    loss_rows = loss_place.shape[0] // groups
    vocab_rows, slice_width = embed_table.shape
    vocab_live = min(groups * vocab_rows, VOCAB_REAL)
    model_dim = layer_weight.shape[1]
    hidden_units = small_params.shape[0] - 10 * model_dim
    head_width = model_dim // part_count
    length = part_count * tok_rows
    (
        bias_q,
        bias_v,
        bias_out,
        bias_up,
        bias_down,
        gain_one,
        shift_one,
        gain_two,
        shift_two,
        gain_final,
        shift_final,
    ) = pieces(small_params, model_dim, hidden_units)

    at_a, at_b = lax.axis_index("za"), lax.axis_index("zb")
    order = Order()
    weight_low = layer_weight.astype(jnp.bfloat16)
    gathered = lax.all_gather(weight_low, ALL, axis=0, tiled=True)
    table_low = embed_table.astype(jnp.bfloat16)
    other_low = swap(table_low, "zb")
    far_low = swap(table_low, "y")
    pair = in_order(at_b, table_low, other_low, 0)
    table_near = in_order(at_c, pair, swap(pair, "core"), 1)

    pair_rows = 2 * vocab_rows
    pair_range = jnp.arange(pair_rows, dtype=jnp.int32)
    plane_step = 2 * ways * vocab_rows
    first_start = (group_id - at_b * 2 * ways) * vocab_rows

    def in_pair(ids):
        one, two = ids - first_start, ids - first_start - plane_step
        inside = (one >= 0) & (one < vocab_rows)
        both = (two >= 0) & (two < vocab_rows)
        return jnp.where(inside, one, jnp.where(both, two + vocab_rows, -1))

    def of_this_b(tensor):
        return pick(tensor.reshape(2, 2, ways, 2, -1, tensor.shape[-1]), at_b, 1)

    own_ids = own_first(own_first(of_this_b(token_ids), at_a, 0), at_x, 2)
    near_ids = in_order(at_c, own_ids, swap(own_ids, "core"), 4)
    all_ids = in_order(at_y, near_ids, swap(near_ids, "y"), 4).swapaxes(3, 4)

    def looked_up(ids, rows_of):
        hot = (in_pair(ids).reshape(-1, 1) == pair_range[None, :]).astype(jnp.bfloat16)
        got = plain_dot(hot, rows_of).astype(jnp.bfloat16)
        return got.reshape(2, ways, tok_rows, -1)

    near = [looked_up(own_ids[at], table_near) for at in (1, 0)]
    near = over_x(*near)
    far_low = order.hold(far_low, near)
    far_other = order.hold(swap(other_low, "y"), near)
    pair = in_order(at_b, far_low, far_other, 0)
    table_far = in_order(at_c, pair, swap(pair, "core"), 1)
    far = [looked_up(own_ids[at], table_far) for at in (1, 0)]
    far = over_x(*far)
    half_near = added(near[0], swap(near[1], "za"))
    half_far = added(far[0], swap(far[1], "za"))
    embedded = in_order(at_y, half_near, half_far, 1)
    table_full = in_order(at_y, table_near, table_far, 1)

    group_lengths = jnp.take(lengths, group_id, axis=0)
    bounds = jnp.cumsum(group_lengths)[:-1]
    positions = jnp.arange(length, dtype=jnp.int32)
    starts = jnp.max(
        jnp.where(positions[:, None] >= bounds[None, :], bounds[None, :], 0), 1
    ).astype(jnp.int32)[None]

    normed_low = layer_norm(embedded, gain_one, shift_one).astype(jnp.bfloat16)
    bias_joined = jnp.concatenate([bias_q, jnp.zeros_like(bias_q), bias_v])[None]
    joined = join(normed_low, gathered, bias_joined, part_count)
    joined = lax.all_to_all(joined, SEQ, split_axis=0, concat_axis=0, tiled=True)
    mixture, mixture_wide, logsum = attend(starts, joined)
    mixed_low = lax.all_to_all(mixture, SEQ, split_axis=0, concat_axis=0, tiled=True)
    mixed_low = mixed_low.swapaxes(0, 1).reshape(tok_rows, model_dim)
    project_out = gathered[3 * model_dim : 4 * model_dim]
    expand_weight = gathered[4 * model_dim : 4 * model_dim + hidden_units]
    reduce_weight = gathered[4 * model_dim + hidden_units :]
    middle = embedded + low_dot(mixed_low, project_out) + bias_out
    normed_two_low = layer_norm(middle, gain_two, shift_two).astype(jnp.bfloat16)
    hidden = low_dot(normed_two_low, expand_weight) + bias_up
    active_low = smooth(hidden).astype(jnp.bfloat16)
    residual_out = middle + plain_dot(active_low, reduce_weight) + bias_down
    final_out = layer_norm(residual_out, gain_final, shift_final)
    own_pos = lax.dynamic_slice_in_dim(loss_place[:, 0], group_id * loss_rows, loss_rows, 0)
    pos_hot = own_pos[:, None] == jnp.arange(tok_rows, dtype=jnp.int32)[None, :]
    chosen = plain_dot(pos_hot.astype(jnp.bfloat16), final_out.astype(jnp.bfloat16)).astype(
        jnp.bfloat16
    )

    head_rows = in_order(at_a, chosen[None], swap(chosen, "za")[None], 0)
    head_rows = in_order(at_x, head_rows[None], swap(head_rows, "x")[None], 0)
    if ways > 1:
        head_rows = lax.all_gather(head_rows, "w", axis=0, tiled=False)
    head_rows = head_rows.reshape(-1, model_dim)

    def of_rows(tensor):
        return lax.optimization_barrier(of_this_b(tensor).transpose(1, 2, 0, 3, 4).reshape(-1))

    logits = low_dot(head_rows, table_full)
    if groups * vocab_rows > vocab_live:
        live = jnp.minimum(vocab_live - first_start, vocab_rows)
        live_two = vocab_live - first_start - plane_step
        kept = jnp.where(pair_range < vocab_rows, pair_range < live, pair_range - vocab_rows < live_two)
        logits = jnp.where(kept[None, :], logits, MASKED)
    target_hot = pair_range[None, :] == lax.optimization_barrier(in_pair(of_rows(targets)))[:, None]
    target_part = jnp.sum(jnp.where(target_hot, logits, 0.0), 1)
    local_peak = jnp.max(logits, 1)
    local_sum = jnp.sum(jnp.exp(logits - local_peak[:, None]), 1)
    sums = jnp.stack([local_peak, local_sum, target_part])

    def merged(one, two):
        peak = jnp.maximum(one[0], two[0])
        summed = one[1] * jnp.exp(one[0] - peak) + two[1] * jnp.exp(two[0] - peak)
        return jnp.stack([peak, summed, one[2] + two[2]])

    for name in ("za", "x"):
        sums = merged(sums, swap(sums, name))
    if ways > 1:
        everyone = lax.all_gather(sums, "w", axis=0, tiled=False)
        sums = everyone[0]
        for way in range(1, ways):
            sums = merged(sums, everyone[way])
    logsum_all = sums[0] + jnp.log(sums[1])
    target_logit = sums[2]
    weight_rows = of_rows(loss_flag).astype(jnp.float32)
    chance = jnp.exp(logits - logsum_all[:, None])
    grad_logits = weight_rows[:, None] * (chance - target_hot.astype(jnp.float32))
    grad_low = grad_logits.astype(jnp.bfloat16)
    grad_rows = plain_dot(grad_low, table_full).astype(jnp.bfloat16)
    grad_rows = grad_rows.reshape(ways, 2, 2, loss_rows, model_dim)
    grad_rows = [pick(grad_rows, side, 1).swapaxes(0, 1) for side in (1 - at_x, at_x)]
    grad_chosen = over_x(*grad_rows)
    grad_chosen = added(pick(grad_chosen, at_a), swap(pick(grad_chosen, 1 - at_a), "za"))

    def table_part(by_y, by_c):
        place = (at_y ^ by_y) * 2 + (at_c ^ by_c)
        cols = lax.dynamic_slice_in_dim(head_rows, place * slice_width, slice_width, 1)
        return outer_dot(grad_low, cols).astype(jnp.bfloat16)

    far_sum = lowered(table_part(1, 0), swap(table_part(1, 1), "core"))
    near_sum = added(table_part(0, 0), swap(table_part(0, 1), "core"))
    grad_chosen = order.hold(grad_chosen, near_sum, far_sum, all_ids)
    head_table_grad = added(near_sum, swap(far_sum, "y"))

    grad_final = lax.dot_general(
        pos_hot.astype(jnp.float32),
        grad_chosen,
        (((0,), (0,)), ((), ())),
        precision=HIGHEST,
        preferred_element_type=jnp.float32,
    )

    is_first = group_id == 2 * ways * at_b
    loss_part = jnp.where(is_first, jnp.sum(weight_rows * (logsum_all - target_logit)), 0.0)
    count_part = jnp.where(is_first, jnp.sum(weight_rows), 0.0)
    unused, final_back = jax.vjp(layer_norm, residual_out, gain_final, shift_final)
    grad_resid, grad_gain_final, grad_shift_final = final_back(grad_final)
    resid_low = grad_resid.astype(jnp.bfloat16)
    grad_bias_down = column_sum(resid_low)
    plane_rows = layer_weight.shape[0] * groups * part_count // PLANES
    reduce_cut = hidden_units - plane_rows
    plane_three = outer_dot(active_low[:, reduce_cut:], resid_low, jnp.bfloat16)
    piece_three = reduce_planes(by_owner(plane_three, 1))
    resid_low = order.hold(resid_low, plane_three)
    grad_active = low_dot(resid_low, reduce_weight)
    unused, gelu_back = jax.vjp(smooth, hidden)
    hidden_low = gelu_back(grad_active)[0].astype(jnp.bfloat16)
    grad_bias_up = column_sum(hidden_low)
    hidden_low = order.hold(hidden_low, head_table_grad)
    unused, two_back = jax.vjp(layer_norm, middle, gain_two, shift_two)
    grad_middle_part, grad_gain_two, grad_shift_two = two_back(plain_dot(hidden_low, expand_weight))
    grad_middle = grad_resid + grad_middle_part
    middle_low = grad_middle.astype(jnp.bfloat16)
    grad_bias_out = column_sum(middle_low)
    grad_mixed = plain_dot(middle_low, project_out)
    grad_heads = lax.all_to_all(
        grad_mixed.astype(jnp.bfloat16).reshape(tok_rows, part_count, head_width).swapaxes(0, 1),
        SEQ,
        split_axis=0,
        concat_axis=0,
        tiled=True,
    )
    def once(*earlier):
        return lambda tensor: order.hold(tensor, *earlier)

    between = by_owner(
        jnp.concatenate(
            [
                outer_dot(middle_low, mixed_low, jnp.bfloat16),
                outer_dot(hidden_low, normed_two_low, jnp.bfloat16),
                outer_dot(active_low[:, :reduce_cut], resid_low, jnp.bfloat16),
            ],
            0,
        ),
        2,
    )
    pieces_between = reduce_planes(between)
    grad_heads = order.hold(grad_heads, between)
    grad_joined = attend_back(starts, joined, grad_heads, mixture_wide, logsum)
    grad_joined = lax.all_to_all(grad_joined, SEQ, split_axis=0, concat_axis=0, tiled=True)
    grad_joined = order.hold(grad_joined, piece_three)
    grad_joined = grad_joined.transpose(2, 1, 0, 3).reshape(tok_rows, 3 * model_dim)
    core_zero = scatter_core(outer_dot(grad_joined, normed_low, jnp.bfloat16))
    unused, one_back = jax.vjp(layer_norm, embedded, gain_one, shift_one)
    grad_embed_part, grad_gain_one, grad_shift_one = one_back(
        plain_dot(grad_joined, gathered[: 3 * model_dim])
    )
    rows_back = (grad_middle + grad_embed_part).astype(jnp.bfloat16)
    rows_back = lax.all_to_all(rows_back, SEQ, split_axis=1, concat_axis=0, tiled=True)
    grad_bias_q = column_sum(grad_joined[:, :model_dim])
    grad_bias_v = column_sum(grad_joined[:, 2 * model_dim :])
    rows_back = rows_back.reshape(2, length // 2, slice_width)

    from_all = [from_groups(rows_back[0])]
    first_zero = scatter_first(order.hold(core_zero, rows_back))
    from_all.append(from_groups(order.hold(rows_back[1], core_zero), once(first_zero)))
    second_zero = scatter_second(first_zero, once(from_all[0]))
    piece_zero = scatter_last(second_zero, once(from_all[1]))
    totals = jnp.concatenate(
        [
            grad_bias_q,
            grad_bias_v,
            grad_bias_out,
            grad_bias_up,
            grad_bias_down,
            grad_gain_one,
            grad_shift_one,
            grad_gain_two,
            grad_shift_two,
            grad_gain_final,
            grad_shift_final,
            jnp.stack([loss_part, count_part]),
        ]
    )
    totals = total_of(order.hold(totals, from_all[1]))
    small_grad, loss_sum, loss_count = totals[:-2], totals[-2], totals[-1]
    row_range = jnp.arange(vocab_rows, dtype=jnp.int32)[:, None]
    sides = {"mine": at_b, "theirs": 1 - at_b}
    spread = {
        name: lax.dynamic_slice_in_dim(head_table_grad, side * vocab_rows, vocab_rows, 0)
        for name, side in sides.items()
    }
    id_halves = all_ids.reshape(2, 2, ways, 2, length // 2)
    for at in range(2):
        got = from_all[at].reshape(-1, slice_width)
        ids = id_halves[:, :, :, at].reshape(1, -1) - first_start
        for name, side in sides.items():
            hot = (row_range == ids - side * plane_step).astype(jnp.bfloat16)
            spread[name] = spread[name] + plain_dot(hot, got)
    table_grad = added(spread["mine"], swap(spread["theirs"].astype(jnp.bfloat16), "zb"))
    quarters = jnp.concatenate([piece_zero[None], pieces_between, piece_three], 0)
    layer_grad = jnp.stack(sent_z([pick(quarters, plane) for plane in planes_from_here()]))
    squares = total_at_once(
        jnp.sum(jnp.square(layer_grad.astype(jnp.float32))) + jnp.sum(table_grad * table_grad)
    )
    loss_count = loss_count + order.zero()
    gradient_norm = jnp.sqrt(squares + jnp.sum(small_grad * small_grad))
    factor = 1.0 / jnp.maximum(gradient_norm, 1.0)
    out_bias_grad = factor * small_grad[2 * model_dim : 3 * model_dim]
    layer_next, layer_first_next, layer_second_next, basis_next, stat_next = rotated_update(
        layer_weight, layer_first, layer_second, layer_grad, factor, stat_matrix, rot_basis
    )
    small_next, small_first_next, small_second_next = adam_update(
        small_params, small_first, small_second, factor * small_grad, RATE_SMALL
    )
    table_next, table_first_next, table_second_next = adam_update(
        embed_table, table_first, table_second, factor * table_grad, RATE_TABLE
    )
    return (
        loss_sum,
        loss_count,
        gradient_norm,
        layer_next,
        layer_first_next,
        layer_second_next,
        basis_next,
        stat_next,
        small_next,
        small_first_next,
        small_second_next,
        table_next,
        table_first_next,
        table_second_next,
        out_bias_grad,
    )


def solution(mesh):
    vocab, seq = mesh.shape["vocab"], mesh.shape["seq"]
    inner = Mesh(mesh.devices.reshape(2, 2, vocab // 8, 2, seq // 2, 2), ALL)
    in_specs = (
        P(None, SEQ),
        P(),
        P(None, SEQ),
        P(None, SEQ),
        P(None, SEQ),
        P(ALL, None),
        P(ALL, None),
        P(ALL, None),
        P(ALL, None, None, None),
        P(ALL, None, None, None),
        P(),
        P(),
        P(),
        P(VOCAB, SEQ),
        P(VOCAB, SEQ),
        P(VOCAB, SEQ),
    )
    out_specs = (
        P(),
        P(),
        P(),
        P(ALL, None),
        P(ALL, None),
        P(ALL, None),
        P(ALL, None, None, None),
        P(ALL, None, None, None),
        P(),
        P(),
        P(),
        P(VOCAB, SEQ),
        P(VOCAB, SEQ),
        P(VOCAB, SEQ),
        P(),
    )
    return jax.shard_map(body, mesh=inner, in_specs=in_specs, out_specs=out_specs, check_vma=False)
```

```python
from functools import partial

import jax
import jax.numpy as jnp
from jax import lax
from jax.experimental import pallas as pl
from jax.experimental.pallas import tpu as pltpu
from jax.sharding import Mesh, PartitionSpec as P

HEAD_SIZE = 64
VOCAB_REAL = 50257
STEP = 5


NORM_EPS = 1e-05
BETA_ONE = 0.9
BETA_TWO = 0.95
BETA_STAT = 0.95
ADAM_EPS = 1e-08
WEIGHT_DECAY = 0.1
RATE_LAYER = 0.025
RATE_SMALL = 0.08
RATE_TABLE = 0.04
MASKED = -1e30
HIGHEST = lax.Precision.HIGHEST
LANES_BOTH = (((1,), (1,)), ((), ()))
PLANE = ("za", "zb")
VOCAB = PLANE + ("w", "x")
SEQ = ("y", "core")
ALL = VOCAB + SEQ
OWNERS = ("w", "x", "y", "core")
PLANES = 4


def layer_norm(inputs, gain, shift):
    centre = inputs - jnp.mean(inputs, -1, keepdims=True)
    spread = jnp.mean(centre * centre, -1, keepdims=True)
    return centre * lax.rsqrt(spread + NORM_EPS) * (1.0 + gain) + shift


def smooth(inputs):
    return jax.nn.gelu(inputs, approximate=True)


def low_dot(left, right):
    return lax.dot_general(left, right, LANES_BOTH, preferred_element_type=jnp.float32)


def plain_dot(left, right):
    return jnp.dot(left, right, preferred_element_type=jnp.float32)


def outer_dot(left, right, kind=jnp.float32):
    return lax.dot_general(left, right, (((0,), (0,)), ((), ())), preferred_element_type=kind)


def column_sum(values):
    return jnp.sum(values.astype(jnp.float32), 0)


def pieces(small_params, model_dim, hidden_units):
    bounds = [0, model_dim, 2 * model_dim, 3 * model_dim, 3 * model_dim + hidden_units]
    for place_id in range(7):
        bounds.append(bounds[-1] + model_dim)
    return [small_params[bounds[place_id] : bounds[place_id + 1]] for place_id in range(11)]


def swap(tensor, axis):
    return lax.ppermute(tensor, axis, [(0, 1), (1, 0)])


def shift(tensor, step):
    step %= PLANES
    if step == 0:
        return tensor
    return lax.ppermute(tensor, PLANE, [(i, (i + step) % PLANES) for i in range(PLANES)])


def planes_from_here():
    return [(lax.axis_index(PLANE) + step) % PLANES for step in range(PLANES)]


def gathered_z(tensor):
    return [shift(tensor, -step) for step in range(PLANES)]


def sent_z(terms):
    return [shift(terms[step], step) for step in range(PLANES)]


def pick(tensor, place, axis=0):
    return lax.dynamic_index_in_dim(tensor, place, axis, keepdims=False)


def added(*tensors):
    total = tensors[0].astype(jnp.float32)
    for tensor in tensors[1:]:
        total = total + tensor.astype(jnp.float32)
    return total


def lowered(*tensors):
    return added(*tensors).astype(jnp.bfloat16)


def in_order(place, own, other, axis):
    return jnp.where(
        place == 0, jnp.concatenate([own, other], axis), jnp.concatenate([other, own], axis)
    )


class Order:
    def __init__(self):
        self.marks = []

    def hold(self, tensors, *earlier):
        marks = [lax.slice(t, (0,) * t.ndim, (1,) * t.ndim).reshape(()) for t in earlier]
        tensors, *marks = lax.optimization_barrier((tensors, *marks))
        self.marks += [mark.astype(jnp.float32) for mark in marks]
        return tensors

    def zero(self):
        return sum(0.0 * mark for mark in self.marks)


def flip(tensor, by_core):
    pairs = []
    for place in range(8):
        pairs.append((place, place ^ (4 if by_core[place % 2] == "x" else 2)))
    return lax.ppermute(tensor, ("x", "y", "core"), pairs)


def by_owner(grads, planes):
    shape = (planes, lax.axis_size(ALL), -1, grads.shape[1])
    return lax.optimization_barrier(grads.reshape(shape).swapaxes(0, 1))


def reduce_planes(grads):
    return lax.psum_scatter(grads, OWNERS + PLANE, scatter_dimension=0, tiled=False)


def as_is(tensor):
    return tensor


def scatter_core(grads, wait=as_is):
    model_dim = grads.shape[1]
    at_c = lax.axis_index("core")
    shaped = grads.reshape(lax.axis_size("w"), 2, 2, 2, -1, model_dim)
    return lowered(pick(shaped, at_c, 3), wait(swap(pick(shaped, 1 - at_c, 3), "core")))


def scatter_first(shaped, wait=as_is):
    at_x, at_y, at_c = (lax.axis_index(name) for name in ("x", "y", "core"))
    ways, unused, unused, rows, model_dim = shaped.shape
    shaped = shaped.reshape(ways, 4, rows, model_dim)

    def half(x, y):
        spots = (jnp.where(at_c == 0, y, 2 * x), jnp.where(at_c == 0, 2 + y, 2 * x + 1))
        return jnp.stack([pick(shaped, spot, 1) for spot in spots], 1)

    return lowered(half(at_x, at_y), wait(flip(half(1 - at_x, 1 - at_y), "yx")))


def scatter_second(pair, wait=as_is):
    spot = jnp.where(lax.axis_index("core") == 0, lax.axis_index("x"), lax.axis_index("y"))
    own = lowered(pick(pair, spot, 1), wait(flip(pick(pair, 1 - spot, 1), "xy")))
    if lax.axis_size("w") > 1:
        own = lax.psum_scatter(own, "w", scatter_dimension=0, tiled=True)
    return own[0]


def scatter_last(own, wait=as_is):
    rows, model_dim = own.shape
    quarters = own.reshape(PLANES, rows // PLANES, model_dim)
    got = sent_z([pick(quarters, plane) for plane in planes_from_here()])
    return lowered(got[0], *[wait(part) for part in got[1:]])


def own_first(tensor, place, axis):
    return jnp.stack([pick(tensor, place, axis), pick(tensor, 1 - place, axis)])


def over_x(theirs, mine):
    both = lowered(mine, swap(theirs, "x"))
    if lax.axis_size("w") > 1:
        return lax.psum_scatter(both, "w", scatter_dimension=1, tiled=False)
    return both[:, 0]


def from_groups(tensor, wait=as_is):
    if lax.axis_size("w") > 1:
        tensor = lax.all_gather(tensor, "w", axis=0, tiled=False)
    else:
        tensor = tensor[None]
    both = [tensor, wait(swap(tensor, "za"))]
    return jnp.stack(both + [swap(part, "x") for part in both]).reshape((2, 2) + tensor.shape)


def total_of(values):
    for name in ("core", "y", "x", "zb", "za"):
        values = values + swap(values, name)
    return lax.psum(values, "w") if lax.axis_size("w") > 1 else values


def total_at_once(value):
    spread = jnp.broadcast_to(value, (lax.axis_size(ALL), 1))
    return jnp.sum(lax.all_to_all(spread, ALL, split_axis=0, concat_axis=0, tiled=True))


def _groups(width):
    return [(at,min(128,width-at)) for at in range(0,width,128)]

def _head_part(rows, at, wide):
    lane=lax.broadcasted_iota(jnp.int32,rows.shape,1)
    return jnp.where((lane>=at)&(lane<at+wide),rows,jnp.zeros_like(rows))

def attend_kernel(start_ref, q_ref, k_ref, v_ref, low_ref, out_ref, lse_ref, vt_ref):
    block=q_ref.shape[2]
    step=pl.program_id(0)
    width=q_ref.shape[3]
    for at,wide in _groups(width):
        @pl.when(step==0)
        def _():
            for part in range(v_ref.shape[0]):
                vt_ref[part,at:at+wide,:]=v_ref[part,0,:,at:at+wide].astype(jnp.float32).T.astype(jnp.bfloat16)
    start=start_ref[...]
    sub=lax.broadcasted_iota(jnp.int32,(block,block),0)
    lane=lax.broadcasted_iota(jnp.int32,(block,block),1)
    groups=_groups(width)
    heads=[(at,h) for at,wide in groups for h in range(wide//HEAD_SIZE)]
    parts=[]
    for at,wide in groups:
        queries=q_ref[0,0,:,at:at+wide]*jnp.bfloat16(HEAD_SIZE**-0.5)
        parts+=[_head_part(queries,h*HEAD_SIZE,HEAD_SIZE) for h in range(wide//HEAD_SIZE)]
    def chunk(place, carry, diag):
        offset=place*block
        allowed=sub>=start-offset
        if diag:
            allowed=allowed&(sub<=lane)
        fresh=[]
        scored=[]
        for i,(at,h) in enumerate(heads):
            keys=k_ref[place,0,:,at:min(at+128,width)]
            scores=lax.dot_general(keys,parts[i],LANES_BOTH,preferred_element_type=jnp.float32)
            scored.append(jnp.where(allowed,scores,MASKED))
        for i,(at,h) in enumerate(heads):
            peak,total,acc=carry[i]
            scores=scored[i]
            higher=jnp.maximum(peak,jnp.max(scores,0,keepdims=True))
            raised=jnp.exp(scores-higher)
            shrink=jnp.exp(peak-higher)
            vt=vt_ref[place,i*HEAD_SIZE:(i+1)*HEAD_SIZE,:]
            acc=acc*shrink+jnp.dot(vt,raised.astype(jnp.bfloat16),preferred_element_type=jnp.float32)
            fresh.append((higher,total*shrink+jnp.sum(raised,0,keepdims=True),acc))
        return tuple(fresh)
    carry=tuple((jnp.full((1,block),MASKED,jnp.float32),jnp.zeros((1,block),jnp.float32),jnp.zeros((HEAD_SIZE,block),jnp.float32)) for h in heads)
    carry=lax.fori_loop(0,step,lambda c,x:chunk(c,x,False),carry)
    carry=chunk(step,carry,True)
    for at,wide in groups:
        own=carry[at//HEAD_SIZE:(at+wide)//HEAD_SIZE]
        mixed=jnp.concatenate([acc*(1.0/total) for peak,total,acc in own],0).T
        out_ref[0,:,at:at+wide]=mixed
        low_ref[0,:,at:at+wide]=mixed.astype(jnp.bfloat16)
    for i in range(len(heads)):
        peak,total,acc=carry[i]
        lse_ref[i:i+1,:]=peak+jnp.log(total)

def attend(start, joined):
    parts,_,block,width=joined.shape
    length=parts*block
    rows=lambda i:(i,0,0)
    cols=lambda i:(0,i)
    one=pl.BlockSpec((1,1,block,width),lambda i:(i,0,0,0))
    every=[pl.BlockSpec((parts,1,block,width),lambda i,at=at:(0,at,0,0)) for at in (1,2)]
    return pl.pallas_call(
        attend_kernel,
        grid=(parts,),
        in_specs=[pl.BlockSpec((1,block),cols),one]+every,
        out_specs=[pl.BlockSpec((1,block,width),rows),pl.BlockSpec((1,block,width),rows),pl.BlockSpec((8,block),cols)],
        out_shape=[jax.ShapeDtypeStruct((parts,block,width),jnp.bfloat16),jax.ShapeDtypeStruct((parts,block,width),jnp.float32),jax.ShapeDtypeStruct((8,length),jnp.float32)],
        scratch_shapes=[pltpu.VMEM((parts,width,block),jnp.bfloat16)],
        compiler_params=pltpu.CompilerParams(vmem_limit_bytes=40<<20,dimension_semantics=("arbitrary",)),
    )(start,joined,joined,joined)

def attend_back_kernel(start_ref, q_ref, k_ref, v_ref, do_ref, out_ref, lse_ref, grad_ref, kt_ref, dka_ref, dva_ref):
    block=q_ref.shape[2]
    step=pl.program_id(0)
    width=q_ref.shape[3]
    @pl.when(step==0)
    def _():
        for at,wide in _groups(width):
            for part in range(k_ref.shape[0]):
                kt_ref[part,at:at+wide,:]=k_ref[part,0,:,at:at+wide].astype(jnp.float32).T.astype(jnp.bfloat16)
        dka_ref[...]=jnp.zeros_like(dka_ref)
        dva_ref[...]=jnp.zeros_like(dva_ref)
    start=start_ref[...]
    sub=lax.broadcasted_iota(jnp.int32,(block,block),0)
    lane=lax.broadcasted_iota(jnp.int32,(block,block),1)
    temper=HEAD_SIZE**-0.5
    for at,wide in _groups(width):
        queries=q_ref[0,0,:,at:at+wide]*jnp.bfloat16(temper)
        grads=do_ref[0,:,at:at+wide]
        heads=range(wide//HEAD_SIZE)
        parts=[_head_part(queries,h*HEAD_SIZE,HEAD_SIZE) for h in heads]
        dparts=[_head_part(grads,h*HEAD_SIZE,HEAD_SIZE) for h in heads]
        crossed=(grads.astype(jnp.float32)*out_ref[0,:,at:at+wide]).T
        deltas=[jnp.sum(crossed[h*HEAD_SIZE:(h+1)*HEAD_SIZE],0,keepdims=True) for h in heads]
        lses=[lse_ref[at//HEAD_SIZE+h:at//HEAD_SIZE+h+1,:] for h in heads]
        def chunk(place, carry, diag):
            offset=place*block
            keys=k_ref[place,0,:,at:at+wide]
            values=v_ref[place,0,:,at:at+wide]
            allowed=sub>=start-offset
            if diag:
                allowed=allowed&(sub<=lane)
            fresh=[]
            dkey=None
            for h in heads:
                scores=lax.dot_general(keys,parts[h],LANES_BOTH,preferred_element_type=jnp.float32)
                chance=jnp.exp(jnp.where(allowed,scores,MASKED)-lses[h])
                dchance=lax.dot_general(values,dparts[h],LANES_BOTH,preferred_element_type=jnp.float32)
                dscores=(chance*(dchance-deltas[h])).astype(jnp.bfloat16)
                one=jnp.dot(dscores,parts[h],preferred_element_type=jnp.float32)
                two=jnp.dot(chance.astype(jnp.bfloat16),dparts[h],preferred_element_type=jnp.float32)
                dkey,dval=(one,two) if dkey is None else (dkey+one,dval+two)
                kt=kt_ref[place,at+h*HEAD_SIZE:at+(h+1)*HEAD_SIZE,:]
                fresh.append(carry[h]+jnp.dot(kt,dscores,preferred_element_type=jnp.float32))
            dka_ref[place,:,at:at+wide]+=dkey
            dva_ref[place,:,at:at+wide]+=dval
            return tuple(fresh)
        carry=tuple(jnp.zeros((HEAD_SIZE,block),jnp.float32) for h in heads)
        carry=lax.fori_loop(0,step,lambda c,x:chunk(c,x,False),carry)
        carry=chunk(step,carry,True)
        grad_ref[step,0,:,at:at+wide]=(jnp.concatenate(carry,0).T*temper).astype(jnp.bfloat16)
    @pl.when(step==pl.num_programs(0)-1)
    def _():
        grad_ref[:,1]=dka_ref[...].astype(jnp.bfloat16)
        grad_ref[:,2]=dva_ref[...].astype(jnp.bfloat16)

def attend_back(start, joined, grad, out, lse):
    parts,_,block,width=joined.shape
    rows=lambda i:(i,0,0)
    cols=lambda i:(0,i)
    one=pl.BlockSpec((1,1,block,width),lambda i:(i,0,0,0))
    every=[pl.BlockSpec((parts,1,block,width),lambda i,at=at:(0,at,0,0)) for at in (1,2)]
    return pl.pallas_call(
        attend_back_kernel,
        grid=(parts,),
        in_specs=[pl.BlockSpec((1,block),cols),one]+every+[pl.BlockSpec((1,block,width),rows),pl.BlockSpec((1,block,width),rows),pl.BlockSpec((8,block),cols)],
        out_specs=pl.BlockSpec(joined.shape,lambda i:(0,0,0,0)),
        out_shape=jax.ShapeDtypeStruct(joined.shape,jnp.bfloat16),
        scratch_shapes=[pltpu.VMEM((parts,width,block),jnp.bfloat16),pltpu.VMEM((parts,block,width),jnp.float32),pltpu.VMEM((parts,block,width),jnp.float32)],
        compiler_params=pltpu.CompilerParams(vmem_limit_bytes=40<<20,dimension_semantics=("arbitrary",)),
    )(start,joined,joined,joined,grad,out,lse)


def join_kernel(rows_ref, weight_ref, bias_ref, out_ref):
    width=out_ref.shape[3]
    joined=lax.dot_general(rows_ref[...],weight_ref[...],LANES_BOTH,preferred_element_type=jnp.float32)
    joined=(joined+bias_ref[...]).astype(jnp.bfloat16)
    for place in range(out_ref.shape[0]):
        out_ref[place,0]=joined[:,place*width:(place+1)*width]


def join(rows, weights, bias, parts):
    count,model_dim=rows.shape
    width=model_dim//parts
    pairs=parts//2
    return pl.pallas_call(
        join_kernel,
        grid=(3,pairs),
        in_specs=[pl.BlockSpec((count,model_dim),lambda p,h:(0,0)),
                  pl.BlockSpec((2*width,model_dim),lambda p,h:(p*pairs+h,0)),
                  pl.BlockSpec((1,2*width),lambda p,h:(0,p*pairs+h))],
        out_specs=pl.BlockSpec((2,1,count,width),lambda p,h:(h,p,0,0)),
        out_shape=jax.ShapeDtypeStruct((parts,3,count,width),jnp.bfloat16),
        compiler_params=pltpu.CompilerParams(vmem_limit_bytes=40<<20,dimension_semantics=("arbitrary","arbitrary")),
    )(rows,weights,bias)


def frame_kernel(gram_ref, span_ref, out_ref, work_ref):
    count,size,_=gram_ref.shape
    work_ref[...]=gram_ref[...]
    out_ref[...]=span_ref[...]
    rows=lax.broadcasted_iota(jnp.int32,(size,size),0)
    sub=lax.broadcasted_iota(jnp.int32,(count,32,size),1)
    def panel(step, unused):
        top=pl.multiple_of(step*32,32)
        left=work_ref[:,pl.ds(top,32),:].reshape(count*32,size)
        left=pltpu.roll(left,(size-top)%size,1).reshape(count,32,size)
        right=out_ref[:,pl.ds(top,32),:]
        for k in range(32):
            column=left[:,:,k:k+1]
            pivot=column[:,k:k+1,:]
            inverse=lax.rsqrt(pivot)
            inverse=inverse*(1.5-0.5*pivot*inverse*inverse)
            row_left=left[:,k:k+1,:]*inverse
            row_right=right[:,k:k+1,:]*inverse
            share=jnp.where(sub>k,column*inverse,0.0)
            left=jnp.where(sub==k,row_left,left-share*row_left)
            right=jnp.where(sub==k,row_right,right-share*row_right)
        out_ref[:,pl.ds(top,32),:]=right
        left=pltpu.roll(left.reshape(count*32,size),top,1).reshape(count,32,size)
        below=rows>=top+32
        @pl.when(step<size//32-1)
        def _():
            for b in range(count):
                for ref,part in ((work_ref,left[b]),(out_ref,right[b])):
                    change=lax.dot_general(left[b],part,(((0,),(0,)),((),())),precision=lax.Precision.HIGHEST,preferred_element_type=jnp.float32)
                    ref[b]=jnp.where(below,ref[b]-change,ref[b])
        return unused
    lax.fori_loop(0,size//32,panel,0)

def frame(gram, span):
    return pl.pallas_call(
        frame_kernel,
        out_shape=jax.ShapeDtypeStruct(gram.shape,jnp.float32),
        scratch_shapes=[pltpu.VMEM(gram.shape,jnp.float32)],
        compiler_params=pltpu.CompilerParams(vmem_limit_bytes=40<<20),
    )(gram,span)


def adam_update(weight, first_mom, second, gradient, step_rate):
    first_mom = BETA_ONE * first_mom + (1.0 - BETA_ONE) * gradient
    second = BETA_TWO * second + (1.0 - BETA_TWO) * gradient * gradient
    direction = (
        first_mom / (1.0 - BETA_ONE**STEP) / (jnp.sqrt(second / (1.0 - BETA_TWO**STEP)) + ADAM_EPS)
    )
    return (weight - step_rate * (direction + WEIGHT_DECAY * weight), first_mom, second)


def precise(left, right, dims):
    return lax.dot_general(
        left, right, (dims, ((), ())), precision=HIGHEST, preferred_element_type=jnp.float32
    )


def pair_basis(basis_ref):
    size = basis_ref.shape[2]
    blocks = range(basis_ref.shape[1])
    nothing = jnp.zeros((size, size), jnp.float32)
    rows = [
        jnp.concatenate([basis_ref[0, at] if at == other else nothing for other in blocks], 1)
        for at in blocks
    ]
    return jnp.concatenate(rows, 0)


def turn_kernel(place_ref, grad_ref, basis_ref, turned_ref, outer_ref):
    gradient = jnp.concatenate(
        [grad_ref[(place_ref[0] + PLANES - piece) % PLANES] for piece in range(PLANES)], 0
    ).astype(jnp.float32)
    turned_ref[...] = precise(gradient, pair_basis(basis_ref), ((1,), (0,)))
    outer = precise(gradient, gradient, ((0,), (0,)))
    size = basis_ref.shape[2]
    for at in range(basis_ref.shape[1]):
        part = slice(at * size, (at + 1) * size)
        outer_ref[at] = outer[part, part]


def turned_gradient(gradient, basis):
    blocks, block_len = basis.shape[1], basis.shape[2]
    quarter = gradient.shape[1]
    rows = PLANES * quarter
    return pl.pallas_call(
        turn_kernel,
        grid=(blocks // 2,),
        in_specs=[
            pl.BlockSpec(memory_space=pltpu.SMEM),
            pl.BlockSpec((PLANES, quarter, 2 * block_len), lambda b: (0, 0, b)),
            pl.BlockSpec((1, 2, block_len, block_len), lambda b: (0, b, 0, 0)),
        ],
        out_specs=[
            pl.BlockSpec((rows, 2 * block_len), lambda b: (0, b)),
            pl.BlockSpec((2, block_len, block_len), lambda b: (b, 0, 0)),
        ],
        out_shape=[
            jax.ShapeDtypeStruct((rows, blocks * block_len), jnp.float32),
            jax.ShapeDtypeStruct((blocks, block_len, block_len), jnp.float32),
        ],
        compiler_params=pltpu.CompilerParams(vmem_limit_bytes=40 << 20),
        cost_estimate=pl.CostEstimate(
            flops=8 * rows * blocks * block_len * block_len,
            bytes_accessed=8 * rows * blocks * block_len,
            transcendentals=0,
        ),
    )(lax.axis_index(PLANE).reshape(1), gradient, basis)


def rotated_kernel(
    factor_ref,
    weight_ref,
    first_ref,
    second_ref,
    turned_ref,
    outer_ref,
    stat_ref,
    basis_ref,
    weight_out,
    first_out,
    second_out,
    stat_out,
    gram_ref,
    span_ref,
):
    factor = factor_ref[0, 0]
    turned = turned_ref[...] * factor
    first_mom = BETA_ONE * first_ref[...] + (1.0 - BETA_ONE) * turned
    second = BETA_TWO * second_ref[...] + (1.0 - BETA_TWO) * turned * turned
    direction = (
        first_mom / (1.0 - BETA_ONE**STEP) / (jnp.sqrt(second / (1.0 - BETA_TWO**STEP)) + ADAM_EPS)
    )
    back = precise(direction, pair_basis(basis_ref), ((1,), (1,)))
    weight = weight_ref[...]
    weight_out[...] = weight - RATE_LAYER * (back + WEIGHT_DECAY * weight)
    first_out[...] = first_mom
    second_out[...] = second
    for at in range(basis_ref.shape[1]):
        clipped = outer_ref[at] * factor * factor
        stat_next = BETA_STAT * stat_ref[0, at] + (1.0 - BETA_STAT) * clipped
        stat_out[0, at] = stat_next
        spanned = precise(stat_next, basis_ref[0, at], ((1,), (0,)))
        turned_span = spanned.T
        span_ref[at] = turned_span
        gram_ref[at] = precise(turned_span, spanned, ((1,), (0,)))


def rotated_update(weight, first_mom, second, turned, outer, factor, stat, basis):
    blocks, block_len = basis.shape[1], basis.shape[2]
    rows = weight.shape[0]
    column = pl.BlockSpec((rows, 2 * block_len), lambda b: (0, b))
    square = pl.BlockSpec((1, 2, block_len, block_len), lambda b: (0, b, 0, 0))
    flat = pl.BlockSpec((2, block_len, block_len), lambda b: (b, 0, 0))
    wide = jax.ShapeDtypeStruct(weight.shape, jnp.float32)
    small = jax.ShapeDtypeStruct((blocks, block_len, block_len), jnp.float32)
    weight_next, first_next, second_next, stat_next, gram, span = pl.pallas_call(
        rotated_kernel,
        grid=(blocks // 2,),
        in_specs=[pl.BlockSpec(memory_space=pltpu.SMEM)] + [column] * 4 + [flat] + [square] * 2,
        out_specs=[column] * 3 + [square] + [flat] * 2,
        out_shape=[wide] * 3 + [jax.ShapeDtypeStruct(stat.shape, jnp.float32)] + [small] * 2,
        compiler_params=pltpu.CompilerParams(vmem_limit_bytes=40 << 20),
    )(factor.reshape(1, 1), weight, first_mom, second, turned, outer, stat, basis)
    solved = frame(gram, span)
    return (weight_next, first_next, second_next, jnp.swapaxes(solved, 1, 2)[None], stat_next)


def body(
    token_ids,
    lengths,
    loss_place,
    targets,
    loss_flag,
    layer_weight,
    layer_first,
    layer_second,
    rot_basis,
    stat_matrix,
    small_params,
    small_first,
    small_second,
    embed_table,
    table_first,
    table_second,
):
    group_id = lax.axis_index(VOCAB)
    groups = lax.axis_size(VOCAB)
    part_count = lax.axis_size(SEQ)
    ways = lax.axis_size("w")
    at_x, at_y, at_c = (lax.axis_index(name) for name in ("x", "y", "core"))
    tok_rows = token_ids.shape[0] // groups
    loss_rows = loss_place.shape[0] // groups
    vocab_rows, slice_width = embed_table.shape
    vocab_live = min(groups * vocab_rows, VOCAB_REAL)
    model_dim = layer_weight.shape[1]
    hidden_units = small_params.shape[0] - 10 * model_dim
    head_width = model_dim // part_count
    length = part_count * tok_rows
    (
        bias_q,
        bias_v,
        bias_out,
        bias_up,
        bias_down,
        gain_one,
        shift_one,
        gain_two,
        shift_two,
        gain_final,
        shift_final,
    ) = pieces(small_params, model_dim, hidden_units)

    at_a, at_b = lax.axis_index("za"), lax.axis_index("zb")
    order = Order()
    weight_low = layer_weight.astype(jnp.bfloat16)
    gathered = lax.all_gather(weight_low, ALL, axis=0, tiled=True)
    table_low = embed_table.astype(jnp.bfloat16)
    other_low = swap(table_low, "zb")
    far_low = swap(table_low, "y")
    pair = in_order(at_b, table_low, other_low, 0)
    table_near = in_order(at_c, pair, swap(pair, "core"), 1)

    pair_rows = 2 * vocab_rows
    pair_range = jnp.arange(pair_rows, dtype=jnp.int32)
    plane_step = 2 * ways * vocab_rows
    first_start = (group_id - at_b * 2 * ways) * vocab_rows

    def in_pair(ids):
        one, two = ids - first_start, ids - first_start - plane_step
        inside = (one >= 0) & (one < vocab_rows)
        both = (two >= 0) & (two < vocab_rows)
        return jnp.where(inside, one, jnp.where(both, two + vocab_rows, -1))

    def of_this_b(tensor):
        return pick(tensor.reshape(2, 2, ways, 2, -1, tensor.shape[-1]), at_b, 1)

    own_ids = own_first(own_first(of_this_b(token_ids), at_a, 0), at_x, 2)
    near_ids = in_order(at_c, own_ids, swap(own_ids, "core"), 4)
    all_ids = in_order(at_y, near_ids, swap(near_ids, "y"), 4).swapaxes(3, 4)

    def looked_up(ids, rows_of):
        hot = (in_pair(ids).reshape(-1, 1) == pair_range[None, :]).astype(jnp.bfloat16)
        got = plain_dot(hot, rows_of).astype(jnp.bfloat16)
        return got.reshape(2, ways, tok_rows, -1)

    near = [looked_up(own_ids[at], table_near) for at in (1, 0)]
    near = over_x(*near)
    far_low = order.hold(far_low, near)
    far_other = order.hold(swap(other_low, "y"), near)
    pair = in_order(at_b, far_low, far_other, 0)
    table_far = in_order(at_c, pair, swap(pair, "core"), 1)
    far = [looked_up(own_ids[at], table_far) for at in (1, 0)]
    far = over_x(*far)
    half_near = added(near[0], swap(near[1], "za"))
    half_far = added(far[0], swap(far[1], "za"))
    embedded = in_order(at_y, half_near, half_far, 1)
    table_full = in_order(at_y, table_near, table_far, 1)

    group_lengths = jnp.take(lengths, group_id, axis=0)
    bounds = jnp.cumsum(group_lengths)[:-1]
    positions = jnp.arange(length, dtype=jnp.int32)
    starts = jnp.max(
        jnp.where(positions[:, None] >= bounds[None, :], bounds[None, :], 0), 1
    ).astype(jnp.int32)[None]

    normed_low = layer_norm(embedded, gain_one, shift_one).astype(jnp.bfloat16)
    bias_joined = jnp.concatenate([bias_q, jnp.zeros_like(bias_q), bias_v])[None]
    joined = join(normed_low, gathered, bias_joined, part_count)
    joined = lax.all_to_all(joined, SEQ, split_axis=0, concat_axis=0, tiled=True)
    mixture, mixture_wide, logsum = attend(starts, joined)
    mixed_low = lax.all_to_all(mixture, SEQ, split_axis=0, concat_axis=0, tiled=True)
    mixed_low = mixed_low.swapaxes(0, 1).reshape(tok_rows, model_dim)
    project_out = gathered[3 * model_dim : 4 * model_dim]
    expand_weight = gathered[4 * model_dim : 4 * model_dim + hidden_units]
    reduce_weight = gathered[4 * model_dim + hidden_units :]
    middle = embedded + low_dot(mixed_low, project_out) + bias_out
    normed_two_low = layer_norm(middle, gain_two, shift_two).astype(jnp.bfloat16)
    hidden = low_dot(normed_two_low, expand_weight) + bias_up
    active_low = smooth(hidden).astype(jnp.bfloat16)
    residual_out = middle + plain_dot(active_low, reduce_weight) + bias_down
    final_out = layer_norm(residual_out, gain_final, shift_final)
    own_pos = lax.dynamic_slice_in_dim(loss_place[:, 0], group_id * loss_rows, loss_rows, 0)
    pos_hot = own_pos[:, None] == jnp.arange(tok_rows, dtype=jnp.int32)[None, :]
    chosen = plain_dot(pos_hot.astype(jnp.bfloat16), final_out.astype(jnp.bfloat16)).astype(
        jnp.bfloat16
    )

    head_rows = in_order(at_a, chosen[None], swap(chosen, "za")[None], 0)
    head_rows = in_order(at_x, head_rows[None], swap(head_rows, "x")[None], 0)
    if ways > 1:
        head_rows = lax.all_gather(head_rows, "w", axis=0, tiled=False)
    head_rows = head_rows.reshape(-1, model_dim)

    def of_rows(tensor):
        return lax.optimization_barrier(of_this_b(tensor).transpose(1, 2, 0, 3, 4).reshape(-1))

    logits = low_dot(head_rows, table_full)
    if groups * vocab_rows > vocab_live:
        live = jnp.minimum(vocab_live - first_start, vocab_rows)
        live_two = vocab_live - first_start - plane_step
        kept = jnp.where(pair_range < vocab_rows, pair_range < live, pair_range - vocab_rows < live_two)
        logits = jnp.where(kept[None, :], logits, MASKED)
    target_hot = pair_range[None, :] == lax.optimization_barrier(in_pair(of_rows(targets)))[:, None]
    target_part = jnp.sum(jnp.where(target_hot, logits, 0.0), 1)
    local_peak = jnp.max(logits, 1)
    local_sum = jnp.sum(jnp.exp(logits - local_peak[:, None]), 1)
    sums = jnp.stack([local_peak, local_sum, target_part])

    def merged(one, two):
        peak = jnp.maximum(one[0], two[0])
        summed = one[1] * jnp.exp(one[0] - peak) + two[1] * jnp.exp(two[0] - peak)
        return jnp.stack([peak, summed, one[2] + two[2]])

    for name in ("za", "x"):
        sums = merged(sums, swap(sums, name))
    if ways > 1:
        everyone = lax.all_gather(sums, "w", axis=0, tiled=False)
        sums = everyone[0]
        for way in range(1, ways):
            sums = merged(sums, everyone[way])
    logsum_all = sums[0] + jnp.log(sums[1])
    target_logit = sums[2]
    weight_rows = of_rows(loss_flag).astype(jnp.float32)
    chance = jnp.exp(logits - logsum_all[:, None])
    grad_logits = weight_rows[:, None] * (chance - target_hot.astype(jnp.float32))
    grad_low = grad_logits.astype(jnp.bfloat16)
    grad_rows = plain_dot(grad_low, table_full).astype(jnp.bfloat16)
    grad_rows = grad_rows.reshape(ways, 2, 2, loss_rows, model_dim)
    grad_rows = [pick(grad_rows, side, 1).swapaxes(0, 1) for side in (1 - at_x, at_x)]
    grad_chosen = over_x(*grad_rows)
    grad_chosen = added(pick(grad_chosen, at_a), swap(pick(grad_chosen, 1 - at_a), "za"))

    def table_part(by_y, by_c):
        place = (at_y ^ by_y) * 2 + (at_c ^ by_c)
        cols = lax.dynamic_slice_in_dim(head_rows, place * slice_width, slice_width, 1)
        return outer_dot(grad_low, cols).astype(jnp.bfloat16)

    far_sum = lowered(table_part(1, 0), swap(table_part(1, 1), "core"))
    near_sum = added(table_part(0, 0), swap(table_part(0, 1), "core"))
    grad_chosen = order.hold(grad_chosen, near_sum, far_sum, all_ids)
    head_table_grad = added(near_sum, swap(far_sum, "y"))

    grad_final = lax.dot_general(
        pos_hot.astype(jnp.float32),
        grad_chosen,
        (((0,), (0,)), ((), ())),
        precision=HIGHEST,
        preferred_element_type=jnp.float32,
    )

    is_first = group_id == 2 * ways * at_b
    loss_part = jnp.where(is_first, jnp.sum(weight_rows * (logsum_all - target_logit)), 0.0)
    count_part = jnp.where(is_first, jnp.sum(weight_rows), 0.0)
    unused, final_back = jax.vjp(layer_norm, residual_out, gain_final, shift_final)
    grad_resid, grad_gain_final, grad_shift_final = final_back(grad_final)
    resid_low = grad_resid.astype(jnp.bfloat16)
    grad_bias_down = column_sum(resid_low)
    plane_rows = layer_weight.shape[0] * groups * part_count // PLANES
    reduce_cut = hidden_units - plane_rows
    plane_three = outer_dot(active_low[:, reduce_cut:], resid_low, jnp.bfloat16)
    piece_three = reduce_planes(by_owner(plane_three, 1))
    resid_low = order.hold(resid_low, plane_three)
    grad_active = low_dot(resid_low, reduce_weight)
    unused, gelu_back = jax.vjp(smooth, hidden)
    hidden_low = gelu_back(grad_active)[0].astype(jnp.bfloat16)
    grad_bias_up = column_sum(hidden_low)
    hidden_low = order.hold(hidden_low, head_table_grad)
    unused, two_back = jax.vjp(layer_norm, middle, gain_two, shift_two)
    grad_middle_part, grad_gain_two, grad_shift_two = two_back(plain_dot(hidden_low, expand_weight))
    grad_middle = grad_resid + grad_middle_part
    middle_low = grad_middle.astype(jnp.bfloat16)
    grad_bias_out = column_sum(middle_low)
    grad_mixed = plain_dot(middle_low, project_out)
    grad_heads = lax.all_to_all(
        grad_mixed.astype(jnp.bfloat16).reshape(tok_rows, part_count, head_width).swapaxes(0, 1),
        SEQ,
        split_axis=0,
        concat_axis=0,
        tiled=True,
    )
    def once(*earlier):
        return lambda tensor: order.hold(tensor, *earlier)

    between = by_owner(
        jnp.concatenate(
            [
                outer_dot(middle_low, mixed_low, jnp.bfloat16),
                outer_dot(hidden_low, normed_two_low, jnp.bfloat16),
                outer_dot(active_low[:, :reduce_cut], resid_low, jnp.bfloat16),
            ],
            0,
        ),
        2,
    )
    pieces_between = reduce_planes(between)
    grad_heads = order.hold(grad_heads, between)
    grad_joined = attend_back(starts, joined, grad_heads, mixture_wide, logsum)
    grad_joined = lax.all_to_all(grad_joined, SEQ, split_axis=0, concat_axis=0, tiled=True)
    grad_joined = order.hold(grad_joined, piece_three)
    grad_joined = grad_joined.transpose(2, 1, 0, 3).reshape(tok_rows, 3 * model_dim)
    core_zero = scatter_core(outer_dot(grad_joined, normed_low, jnp.bfloat16))
    unused, one_back = jax.vjp(layer_norm, embedded, gain_one, shift_one)
    grad_embed_part, grad_gain_one, grad_shift_one = one_back(
        plain_dot(grad_joined, gathered[: 3 * model_dim])
    )
    rows_back = (grad_middle + grad_embed_part).astype(jnp.bfloat16)
    rows_back = lax.all_to_all(rows_back, SEQ, split_axis=1, concat_axis=0, tiled=True)
    grad_bias_q = column_sum(grad_joined[:, :model_dim])
    grad_bias_v = column_sum(grad_joined[:, 2 * model_dim :])
    rows_back = rows_back.reshape(2, length // 2, slice_width)

    from_all = [from_groups(rows_back[0])]
    first_zero = scatter_first(order.hold(core_zero, rows_back))
    from_all.append(from_groups(order.hold(rows_back[1], core_zero), once(first_zero)))
    second_zero = scatter_second(first_zero, once(from_all[0]))
    piece_zero = scatter_last(second_zero, once(from_all[1]))
    totals = jnp.concatenate(
        [
            grad_bias_q,
            grad_bias_v,
            grad_bias_out,
            grad_bias_up,
            grad_bias_down,
            grad_gain_one,
            grad_shift_one,
            grad_gain_two,
            grad_shift_two,
            grad_gain_final,
            grad_shift_final,
            jnp.stack([loss_part, count_part]),
        ]
    )
    totals = total_of(order.hold(totals, from_all[1]))
    small_grad, loss_sum, loss_count = totals[:-2], totals[-2], totals[-1]
    row_range = jnp.arange(vocab_rows, dtype=jnp.int32)[:, None]
    sides = {"mine": at_b, "theirs": 1 - at_b}
    spread = {
        name: lax.dynamic_slice_in_dim(head_table_grad, side * vocab_rows, vocab_rows, 0)
        for name, side in sides.items()
    }
    id_halves = all_ids.reshape(2, 2, ways, 2, length // 2)
    for at in range(2):
        got = from_all[at].reshape(-1, slice_width)
        ids = id_halves[:, :, :, at].reshape(1, -1) - first_start
        for name, side in sides.items():
            hot = (row_range == ids - side * plane_step).astype(jnp.bfloat16)
            spread[name] = spread[name] + plain_dot(hot, got)
    table_grad = added(spread["mine"], swap(spread["theirs"].astype(jnp.bfloat16), "zb"))
    quarters = jnp.concatenate([piece_zero[None], pieces_between, piece_three], 0)
    layer_grad = jnp.stack(sent_z([pick(quarters, plane) for plane in planes_from_here()]))
    turned, outer = turned_gradient(layer_grad, rot_basis)
    squares = total_at_once(
        jnp.sum(jnp.square(layer_grad.astype(jnp.float32))) + jnp.sum(table_grad * table_grad)
    )
    loss_count = loss_count + order.zero()
    gradient_norm = jnp.sqrt(squares + jnp.sum(small_grad * small_grad))
    factor = 1.0 / jnp.maximum(gradient_norm, 1.0)
    out_bias_grad = factor * small_grad[2 * model_dim : 3 * model_dim]
    layer_next, layer_first_next, layer_second_next, basis_next, stat_next = rotated_update(
        layer_weight, layer_first, layer_second, turned, outer, factor, stat_matrix, rot_basis
    )
    small_next, small_first_next, small_second_next = adam_update(
        small_params, small_first, small_second, factor * small_grad, RATE_SMALL
    )
    table_next, table_first_next, table_second_next = adam_update(
        embed_table, table_first, table_second, factor * table_grad, RATE_TABLE
    )
    return (
        loss_sum,
        loss_count,
        gradient_norm,
        layer_next,
        layer_first_next,
        layer_second_next,
        basis_next,
        stat_next,
        small_next,
        small_first_next,
        small_second_next,
        table_next,
        table_first_next,
        table_second_next,
        out_bias_grad,
    )


def solution(mesh):
    vocab, seq = mesh.shape["vocab"], mesh.shape["seq"]
    inner = Mesh(mesh.devices.reshape(2, 2, vocab // 8, 2, seq // 2, 2), ALL)
    in_specs = (
        P(None, SEQ),
        P(),
        P(None, SEQ),
        P(None, SEQ),
        P(None, SEQ),
        P(ALL, None),
        P(ALL, None),
        P(ALL, None),
        P(ALL, None, None, None),
        P(ALL, None, None, None),
        P(),
        P(),
        P(),
        P(VOCAB, SEQ),
        P(VOCAB, SEQ),
        P(VOCAB, SEQ),
    )
    out_specs = (
        P(),
        P(),
        P(),
        P(ALL, None),
        P(ALL, None),
        P(ALL, None),
        P(ALL, None, None, None),
        P(ALL, None, None, None),
        P(),
        P(),
        P(),
        P(VOCAB, SEQ),
        P(VOCAB, SEQ),
        P(VOCAB, SEQ),
        P(),
    )
    return jax.shard_map(body, mesh=inner, in_specs=in_specs, out_specs=out_specs, check_vma=False)
```
